128 devices in a mesh: wide: 32 (over z, x_lo, y), narrow: 4 (over x_hi, core).
Axes of the slice: x: 4 (x_hi: 2, x_lo: 2; x = x_hi * 2 + x_lo), y: 4, z: 4, core: 2. Of those that a mesh axis runs over, the one named last changes fastest.
Arguments:
- features: bfloat16 [524288, 128], P(('wide', 'narrow')), may hold values from -6 to 6
- cotangent: bfloat16 [524288, 256], P(('wide', 'narrow')), may hold values from -6 to 6
- w_self: bfloat16 [128, 256], replicated, may hold values from -0.5 to 0.5
- w_neigh: bfloat16 [128, 256], replicated, may hold values from -0.5 to 0.5
- bias: float32 [256], replicated, may hold values from -4 to 4
- tile_weights: bfloat16 [65536, 128, 128], P(('wide', 'narrow')), may hold values from -0.125 to 0.125
- tile_src: int32 [65536], P(('wide', 'narrow')), may hold values from 0 to 47
- tile_dst: int32 [65536], P(('wide', 'narrow')), may hold values from 0 to 31
- tile_live: int32 [65536], P(('wide', 'narrow')), may hold values 0 or 1
- send_rows: int32 [4096, 32], P(('wide', 'narrow')), may hold values from 0 to 4095
- hub_rows: int32 [1024], P(('wide', 'narrow')), may hold values from 0 to 4095
Outputs:
- hidden: bfloat16 [524288, 256], P(('wide', 'narrow'))
- grad_features: float32 [524288, 128], P(('wide', 'narrow'))
- grad_self: float32 [128, 256], replicated
- grad_neigh: float32 [128, 256], replicated
- grad_bias: float32 [256], replicated
The draws below stay inside these ranges and needn't reach their ends.
All inputs are finite; a program needn't handle non-finite values. No bound on the sum of `tile_live` on one device may be relied on, other than what follows from the above.
Results may differ from the reference program's by a relative error of at most 0.007.
Values may be sent and summed in bfloat16 or wider, within the bound.
A program may use at most 192 MiB of HBM per device.

```python
import jax
import jax.numpy as jnp
from jax import lax

F = 128
H = 256
TILE = 128
NODES_DEV = 4096
TILES_DEV = 512
SLOT = 32
HUB_DEV = 8
DEVS = 128
NODES = 524288
HUBS = 1024
SRC_BLOCKS = 48
N_WIDE = 32
N_NARROW = 4


def plant(array, own_key, least, largest):
    longest = array.shape.index(max(array.shape))
    spots = []
    for shift in (0, 1):
        where = [jax.random.randint(jax.random.fold_in(own_key, axis), (), 0, length) for axis, length in enumerate(array.shape)]
        where[longest] = (where[longest] + shift) % array.shape[longest]
        spots.append(tuple(where))
    return array.at[spots[0]].set(least).at[spots[1]].set(largest)


def levels(stream_key, dims, pieces, low, top_value):
    def one(axis_at, parts):
        heights = jax.random.uniform(jax.random.fold_in(jax.random.fold_in(stream_key, 6), axis_at), (parts,), jnp.float32, low / len(pieces), top_value / len(pieces))
        return jnp.repeat(jnp.exp(heights), dims[axis_at] // parts).reshape((-1,) + (1,) * (len(dims) - axis_at - 1))

    gain = one(*pieces[0])
    for cut in pieces[1:]:
        gain = gain * one(*cut)
    return gain


def noise(rng, extent, width, reach, pieces=(), held_as=jnp.bfloat16):
    values = jax.random.normal(rng, extent, jnp.float32) * width
    if len(pieces) > 0:
        values = levels(rng, extent, pieces, -0.22, 0.18) * values
    return jnp.clip(values, min=-reach, max=reach).astype(held_as)


def setup_inputs(seed: int = 0) -> dict:
    streams_of = jax.random.split(jax.random.key(seed), 12)
    return {
        "features": noise(streams_of[0], (NODES, F), 1.0, 6.0, ((0, 128),)),
        "cotangent": noise(streams_of[1], (NODES, H), 1.0, 6.0, ((0, 128),)),
        "w_self": noise(streams_of[2], (F, H), F ** -0.5, 0.5),
        "w_neigh": noise(streams_of[3], (F, H), F ** -0.5, 0.5),
        "bias": noise(streams_of[4], (H,), 1.0, 4.0, (), jnp.float32),
        "tile_weights": noise(streams_of[5], (DEVS * TILES_DEV, TILE, TILE), (TILE * TILES_DEV * TILE // NODES_DEV) ** -0.5, 0.125, ((0, 128),)),
        "tile_src": plant(jax.random.randint(streams_of[6], (DEVS * TILES_DEV,), 0, SRC_BLOCKS), jax.random.fold_in(streams_of[6], 1), 0, SRC_BLOCKS - 1).astype(jnp.int32),
        "tile_dst": plant(jax.random.randint(streams_of[7], (DEVS * TILES_DEV,), 0, NODES_DEV // TILE), jax.random.fold_in(streams_of[7], 1), 0, (NODES_DEV // TILE) - 1).astype(jnp.int32),
        "tile_live": plant((jax.random.randint(streams_of[8], (DEVS * TILES_DEV,), 0, 4) < 3).astype(jnp.int32), jax.random.fold_in(streams_of[8], 1), 0, 1),
        "send_rows": plant(jax.random.randint(streams_of[9], (DEVS * N_WIDE, SLOT), 0, NODES_DEV), jax.random.fold_in(streams_of[9], 1), 0, NODES_DEV - 1).astype(jnp.int32),
        "hub_rows": plant(jax.random.randint(streams_of[10], (HUBS,), 0, NODES_DEV), jax.random.fold_in(streams_of[10], 1), 0, NODES_DEV - 1).astype(jnp.int32),
    }


def gelu_tanh(value):
    return jax.nn.gelu(value, approximate=True)

def reference(features, cotangent, w_self, w_neigh, bias, tile_weights, tile_src, tile_dst, tile_live, send_rows, hub_rows):
    devs = N_WIDE * N_NARROW
    flat_feat = features
    wide_ids = jnp.arange(N_WIDE, dtype=jnp.int32)
    narrow_ids = jnp.arange(N_NARROW, dtype=jnp.int32)
    sends = send_rows.reshape(N_WIDE, N_NARROW, N_WIDE, SLOT)
    anchor = ((wide_ids[:, None, None, None] * N_NARROW + narrow_ids[None, :, None, None]) * NODES_DEV + sends).astype(jnp.int32)
    sent = flat_feat[anchor]
    received = jnp.transpose(sent, (2, 1, 0, 3, 4)).reshape(devs, N_WIDE * SLOT, F)
    owners = (jnp.arange(HUBS, dtype=jnp.int32) // HUB_DEV).astype(jnp.int32)
    hub_index = (owners * NODES_DEV + hub_rows).astype(jnp.int32)
    hub_features = flat_feat[hub_index]
    feat_dev = features.reshape(devs, NODES_DEV, F)
    cot_dev = cotangent.reshape(devs, NODES_DEV, H)
    tiles_dev = tile_weights.reshape(devs, TILES_DEV, TILE, TILE)
    src_dev = tile_src.reshape(devs, TILES_DEV)
    dst_dev = tile_dst.reshape(devs, TILES_DEV)
    live_dev = tile_live.reshape(devs, TILES_DEV)
    dst_blocks = NODES_DEV // TILE

    def one_device(carry, inputs):
        g_self, g_neigh, g_bias, g_hub = carry
        feat, cot, recv, tiles, src, dst, live = inputs
        buffer = jnp.concatenate([feat, recv, hub_features], axis=0).reshape(SRC_BLOCKS, TILE, F)
        tiles32 = tiles.astype(jnp.float32)
        picked = buffer[src].astype(jnp.float32)
        products = jnp.einsum('tij,tjf->tif', tiles32, picked) * live.astype(jnp.float32)[:, None, None]
        aggregate = jax.ops.segment_sum(products, dst, num_segments=dst_blocks).reshape(NODES_DEV, F).astype(jnp.bfloat16)
        pre = jnp.dot(feat, w_self, preferred_element_type=jnp.float32) + jnp.dot(aggregate, w_neigh, preferred_element_type=jnp.float32) + bias
        hidden = gelu_tanh(pre).astype(jnp.bfloat16)
        _, pullback = jax.vjp(gelu_tanh, pre)
        grad_pre = pullback(cot.astype(jnp.float32))[0].astype(jnp.bfloat16)
        g_self = g_self + jnp.dot(feat.T, grad_pre, preferred_element_type=jnp.float32)
        g_neigh = g_neigh + jnp.dot(aggregate.T, grad_pre, preferred_element_type=jnp.float32)
        g_bias = g_bias + lax.optimization_barrier(jnp.sum(grad_pre.astype(jnp.float32), axis=0))
        grad_agg = jnp.dot(grad_pre, w_neigh.T, preferred_element_type=jnp.float32).astype(jnp.bfloat16)
        back = jnp.einsum('tij,tif->tjf', tiles32, grad_agg.reshape(dst_blocks, TILE, F)[dst].astype(jnp.float32)) * live.astype(jnp.float32)[:, None, None]
        grad_buffer = jax.ops.segment_sum(back, src, num_segments=SRC_BLOCKS).reshape(SRC_BLOCKS * TILE, F)
        own = jnp.dot(grad_pre, w_self.T, preferred_element_type=jnp.float32) + grad_buffer[:NODES_DEV]
        bound = grad_buffer[NODES_DEV:NODES_DEV + N_WIDE * SLOT]
        g_hub = g_hub + grad_buffer[NODES_DEV + N_WIDE * SLOT:]
        return ((g_self, g_neigh, g_bias, g_hub), (hidden, own, bound))
    init = (jnp.zeros((F, H), jnp.float32), jnp.zeros((F, H), jnp.float32), jnp.zeros((H,), jnp.float32), jnp.zeros((HUBS, F), jnp.float32))
    carry, outs = lax.scan(one_device, init, (feat_dev, cot_dev, received, tiles_dev, src_dev, dst_dev, live_dev))
    g_self, g_neigh, g_bias, g_hub = carry
    hidden, own, bound = outs
    grad_features = own.reshape(NODES, F)
    returned = jnp.transpose(bound.reshape(N_WIDE, N_NARROW, N_WIDE, SLOT, F), (2, 1, 0, 3, 4))
    grad_features = grad_features.at[anchor.reshape(-1)].add(returned.reshape(-1, F))
    grad_features = grad_features.at[hub_index].add(g_hub)
    return (hidden.reshape(NODES, H), grad_features, g_self, g_neigh, g_bias)
```

```python
import functools

import jax
import jax.numpy as jnp
from jax import lax
from jax.experimental import pallas as pl
from jax.experimental.pallas import tpu as pltpu
from jax.sharding import PartitionSpec as P

MESH = pl.DeviceIdType.MESH
BF, F32, I32 = jnp.bfloat16, jnp.float32, jnp.int32
TILE = 128
DST = 32
SRC = 48
TILES = 512
SLOTS = 640
UNROLL = 16
ROWS = 1024
CHUNKS = 8
SLOT = 32
HUB = 8
WIDE = 32
NARROW = 4
GELU_A = 0.7978845608028654
GELU_B = 0.044715


def mm(a, b):
    return jnp.dot(a, b, preferred_element_type=F32)


def nt(a, b):
    return lax.dot_general(a, b, (((1,), (1,)), ((), ())), preferred_element_type=F32)


def tn(a, b):
    return lax.dot_general(a, b, (((0,), (0,)), ((), ())), preferred_element_type=F32)


def iota(shape, dim):
    return lax.broadcasted_iota(I32, shape, dim)


def tile_list(key, other, live, keys, zero):
    groups = 64
    hot = jnp.where((iota((groups, TILES), 0) == key) & (live > 0), 1.0, 0.0)
    before = jnp.where(iota((TILES, TILES), 0) < iota((TILES, TILES), 1), 1.0, 0.0).astype(BF)
    rank = mm(hot.astype(BF), before)
    count = jnp.sum(hot, axis=1, keepdims=True).astype(I32)
    even = ((count + 1) // 2 * 2).astype(F32)
    lower = jnp.where(iota((groups, groups), 1) < iota((groups, groups), 0), 1.0, 0.0).astype(BF)
    start = mm(lower, jnp.broadcast_to(even, (groups, TILE)).astype(BF))[:, :1]
    total = jnp.sum(even, axis=0, keepdims=True)
    place = jnp.sum(hot * (rank + start), axis=0, keepdims=True).astype(I32)
    place = jnp.where(live > 0, place, -1)
    at = jnp.where(iota((SLOTS, TILES), 0) == place, 1.0, 0.0).astype(BF)
    t = iota((1, TILES), 1)
    rows = [t // 16, t % 16, other - zero, key - keys]
    row = iota((8, TILES), 0)
    values = jnp.zeros((8, TILES), I32)
    for r, v in enumerate(rows):
        values = jnp.where(row == r, v, values)
    got = nt(values.astype(F32).astype(BF), at).astype(I32)
    pairs = (total * 0.5).astype(I32)
    out = jnp.concatenate(
        [
            got[0:1] * 16 + got[1:2],
            got[2:3] + zero,
            got[3:4] + keys,
            jnp.broadcast_to(pairs, (1, SLOTS)),
        ],
        axis=0,
    )
    return jnp.concatenate([out, out], axis=0)


def fetch_kernel(
    send_rows, hub_rows, feat, src, dst, live, got, list_f, list_b,
    wide32, hubs, picked, msg, near, own, s_row, r_row, s_hub, r_hub, s_near, r_near, s_own,
):
    w = lax.axis_index("wide")
    n = lax.axis_index("narrow")
    barrier = pltpu.get_barrier_semaphore()

    def greet(o, c):
        pl.semaphore_signal(
            barrier, inc=1, device_id=(lax.rem(w + o, WIDE), n), device_id_type=MESH
        )
        return c

    lax.fori_loop(1, WIDE, greet, 0)
    for k in range(1, NARROW):
        pl.semaphore_signal(
            barrier, inc=1, device_id=(w, lax.rem(n + k, NARROW)), device_id_type=MESH
        )

    wide32[...] = feat[...].astype(F32)
    for j in range(HUB):
        hubs[pl.ds(j, 1), :] = wide32[pl.ds(hub_rows[j], 1), :]

    def pick(p, c):
        for j in range(SLOT):
            picked[pl.ds(p * SLOT + j, 1), :] = wide32[pl.ds(send_rows[p, j], 1), :]
        return c

    lax.fori_loop(0, WIDE, pick, 0)
    msg[...] = picked[...].astype(BF)
    near[n] = hubs[...]

    pl.semaphore_wait(barrier, WIDE - 1 + NARROW - 1)

    def near_copy(k, slot):
        return pltpu.make_async_remote_copy(
            src_ref=hubs,
            dst_ref=near.at[slot],
            send_sem=s_near.at[k],
            recv_sem=r_near.at[k],
            device_id=(w, lax.rem(n + k, NARROW)),
            device_id_type=MESH,
        )

    def row_copy(o, slot):
        p = lax.rem(w + o, WIDE)
        return pltpu.make_async_remote_copy(
            src_ref=msg.at[pl.ds(p * SLOT, SLOT)],
            dst_ref=got.at[slot, pl.ds(0, SLOT)],
            send_sem=s_row.at[o],
            recv_sem=r_row.at[o],
            device_id=(p, n),
            device_id_type=MESH,
        )

    def hub_copy(o, slot):
        return pltpu.make_async_remote_copy(
            src_ref=own,
            dst_ref=got.at[slot, pl.ds(SLOT, SLOT)],
            send_sem=s_hub.at[o],
            recv_sem=r_hub.at[o],
            device_id=(lax.rem(w + o, WIDE), n),
            device_id_type=MESH,
        )

    for k in range(1, NARROW):
        near_copy(k, n).start()

    def send_row(o, c):
        row_copy(o, w).start()
        return c

    lax.fori_loop(1, WIDE, send_row, 0)
    mine_row = pltpu.make_async_copy(
        msg.at[pl.ds(w * SLOT, SLOT)], got.at[w, pl.ds(0, SLOT)], s_own.at[0]
    )
    mine_row.start()
    for k in range(1, NARROW):
        near_copy(k, lax.rem(n + NARROW - k, NARROW)).wait_recv()
    own[...] = near[...].reshape(NARROW * HUB, TILE).astype(BF)

    def send_hub(o, c):
        hub_copy(o, w).start()
        return c

    lax.fori_loop(1, WIDE, send_hub, 0)
    mine_hub = pltpu.make_async_copy(own, got.at[w, pl.ds(SLOT, SLOT)], s_own.at[1])
    mine_hub.start()

    def flat(ref):
        return jnp.concatenate([ref[pl.ds(r, 1), :] for r in range(TILES // TILE)], axis=1)

    s, d, l = flat(src), flat(dst), flat(live)
    list_f[...] = tile_list(d, s, l, DST, SRC)
    list_b[...] = tile_list(s, d, l, SRC, DST)

    def finish(o, c):
        slot = lax.rem(w + WIDE - o, WIDE)
        row_copy(o, slot).wait()
        hub_copy(o, slot).wait()
        return c

    lax.fori_loop(1, WIDE, finish, 0)
    for k in range(1, NARROW):
        near_copy(k, n).wait_send()
    mine_row.wait()
    mine_hub.wait()


def fetch(feat, send_rows, hub_rows, src, dst, live):
    smem = pl.BlockSpec(memory_space=pltpu.SMEM)
    vmem = pl.BlockSpec(memory_space=pltpu.VMEM)
    dma = pltpu.SemaphoreType.DMA
    return pl.pallas_call(
        fetch_kernel,
        out_shape=(
            jax.ShapeDtypeStruct((WIDE, 2 * SLOT, TILE), BF),
            jax.ShapeDtypeStruct((8, SLOTS), I32),
            jax.ShapeDtypeStruct((8, SLOTS), I32),
        ),
        in_specs=[smem, smem, vmem, vmem, vmem, vmem],
        out_specs=(pl.BlockSpec(memory_space=pl.ANY), vmem, vmem),
        scratch_shapes=[
            pltpu.VMEM((DST * TILE, TILE), F32),
            pltpu.VMEM((HUB, TILE), F32),
            pltpu.VMEM((WIDE * SLOT, TILE), F32),
            pltpu.VMEM((WIDE * SLOT, TILE), BF),
            pltpu.VMEM((NARROW, HUB, TILE), F32),
            pltpu.VMEM((NARROW * HUB, TILE), BF),
            dma((WIDE,)), dma((WIDE,)), dma((WIDE,)), dma((WIDE,)),
            dma((NARROW,)), dma((NARROW,)), dma((2,)),
        ],
        compiler_params=pltpu.CompilerParams(
            collective_id=0, has_side_effects=True, vmem_limit_bytes=24 * 2**20
        ),
    )(send_rows, hub_rows, feat, src, dst, live)


def layer_kernel(
    list_f, list_b, feat, got, cot, w2, wt2, bias, tiles, hidden, gfeat, bound, msg,
    wbuf, buf, cotb, hidb, gfb, bnb, msb, agg, gt, gbt, wg, gb, sem_t, sem,
):
    quads = TILE // SLOT
    loads = [
        pltpu.make_async_copy(feat, buf.at[pl.ds(0, DST * quads)], sem.at[0]),
        pltpu.make_async_copy(
            got.at[:, pl.ds(0, SLOT)], buf.at[pl.ds(DST * quads, WIDE)], sem.at[1]
        ),
        pltpu.make_async_copy(
            got.at[:, pl.ds(SLOT, SLOT)], buf.at[pl.ds(DST * quads + WIDE, WIDE)], sem.at[2]
        ),
        pltpu.make_async_copy(cot, cotb, sem.at[3]),
    ]
    for c in loads[:3]:
        c.start()
    per = TILES // CHUNKS
    tile_loads = [
        pltpu.make_async_copy(
            tiles.at[pl.ds(i * per, per)], wbuf.at[pl.ds(i * per, per)], sem_t.at[i]
        )
        for i in range(CHUNKS)
    ]
    for c in tile_loads:
        c.start()
    loads[3].start()

    def clear(i, c):
        agg[i] = jnp.zeros((TILE, TILE), F32)
        return c

    lax.fori_loop(0, DST + 1, clear, 0)

    def clear_back(i, c):
        gbt[DST + i] = jnp.zeros((TILE, TILE), F32)
        return c

    lax.fori_loop(0, SRC - DST + 1, clear_back, 0)
    buf[pl.ds(SRC * quads, quads)] = jnp.zeros((quads, SLOT, TILE), BF)
    gt[DST] = jnp.zeros((TILE, TILE), BF)
    gb[...] = jnp.zeros_like(gb)
    wg[...] = jnp.zeros_like(wg)
    for c in loads[:3]:
        c.wait()
    for c in tile_loads:
        c.wait()

    def rows_of(s):
        return buf[pl.ds(s * quads, quads)].reshape(TILE, TILE)

    def forward(i, c):
        parts = []
        for u in range(UNROLL):
            k = 2 * (i * UNROLL + u)
            left = jnp.concatenate([wbuf[list_f[0, k]], wbuf[list_f[0, k + 1]]], axis=1)
            right = jnp.concatenate(
                [rows_of(list_f[1, k]), rows_of(list_f[1, k + 1])], axis=0
            )
            parts.append(mm(left, right))
        for u in range(UNROLL):
            agg[list_f[2, 2 * (i * UNROLL + u)]] += parts[u]
        return c

    lax.fori_loop(0, (list_f[3, 0] + UNROLL - 1) // UNROLL, forward, 0)
    loads[3].wait()
    blocks = ROWS // TILE

    def dense(i, c):
        rows = pl.ds(i * ROWS, ROWS)
        f = buf[pl.ds(i * blocks * quads, blocks * quads)].reshape(ROWS, TILE)
        a = agg[pl.ds(i * blocks, blocks)].reshape(ROWS, TILE).astype(BF)
        x = jnp.concatenate([f, a], axis=1)
        pre = mm(x, w2[...]) + bias[...]
        square = pre * pre
        t = jnp.tanh(pre * (GELU_A + (GELU_A * GELU_B) * square))
        half = 0.5 + 0.5 * t
        hidb[rows, :] = (pre * half).astype(BF)
        slope = half + pre * (0.5 - 0.5 * t * t) * (GELU_A + (3 * GELU_A * GELU_B) * square)
        gp = (cotb[rows, :].astype(F32) * slope).astype(BF)
        wg[...] += tn(x, gp)
        gb[...] += jnp.sum(gp.astype(F32).reshape(ROWS // 8, 8, 2 * TILE), axis=0)
        g2 = nt(wt2[...], gp)
        for j in range(blocks):
            gbt[i * blocks + j] = g2[:TILE, j * TILE : (j + 1) * TILE]
            gt[i * blocks + j] = g2[TILE:, j * TILE : (j + 1) * TILE].astype(BF)
        return c

    lax.fori_loop(0, DST // blocks, dense, 0)
    out_hidden = pltpu.make_async_copy(hidb, hidden, sem.at[4])
    out_hidden.start()

    def backward(i, c):
        parts = []
        for u in range(UNROLL):
            k = 2 * (i * UNROLL + u)
            left = jnp.concatenate([gt[list_b[1, k]], gt[list_b[1, k + 1]]], axis=1)
            right = jnp.concatenate([wbuf[list_b[0, k]], wbuf[list_b[0, k + 1]]], axis=0)
            parts.append(mm(left, right))
        for u in range(UNROLL):
            gbt[list_b[2, 2 * (i * UNROLL + u)]] += parts[u]
        return c

    lax.fori_loop(0, (list_b[3, 0] + UNROLL - 1) // UNROLL, backward, 0)

    def finish_own(i, c):
        gfb[i] = gbt[i].T
        return c

    lax.fori_loop(0, DST, finish_own, 0, unroll=4)
    out_own = pltpu.make_async_copy(gfb, gfeat, sem.at[5])
    out_own.start()
    bias_sum = jnp.sum(gb[...], axis=0, keepdims=True)
    row = iota((16, TILE), 0)
    bias_rows = jnp.where(
        row == 0, bias_sum[:, :TILE], jnp.where(row == 1, bias_sum[:, TILE:], 0.0)
    ).astype(BF)
    for i in range(WIDE * SLOT // TILE):
        bnb[pl.ds(i * quads, quads)] = gbt[DST + i].T.astype(BF).reshape(quads, SLOT, TILE)
        hub = gbt[DST + WIDE * SLOT // TILE + i].T.astype(BF).reshape(quads, SLOT, TILE)
        msb[pl.ds(i * quads, quads), pl.ds(0, SLOT), :] = hub
    for p in range(WIDE):
        part = wg[pl.ds(8 * p, 8), :]
        msb[p, pl.ds(SLOT, 16), :] = jnp.concatenate(
            [part[:, :TILE], part[:, TILE:]], axis=0
        ).astype(BF)
        msb[p, pl.ds(SLOT + 16, 16), :] = bias_rows
    outs = [
        pltpu.make_async_copy(bnb, bound, sem.at[6]),
        pltpu.make_async_copy(msb, msg, sem.at[7]),
    ]
    for c in outs:
        c.start()
    for c in outs:
        c.wait()
    out_own.wait()
    out_hidden.wait()


def layer(list_f, list_b, feat, got, cot, w2, wt2, bias, tiles):
    smem = pl.BlockSpec(memory_space=pltpu.SMEM)
    vmem = pl.BlockSpec(memory_space=pltpu.VMEM)
    hbm = pl.BlockSpec(memory_space=pl.ANY)
    dma = pltpu.SemaphoreType.DMA
    quads = TILE // SLOT
    return pl.pallas_call(
        layer_kernel,
        out_shape=(
            jax.ShapeDtypeStruct((DST * TILE, 2 * TILE), BF),
            jax.ShapeDtypeStruct((DST, TILE, TILE), F32),
            jax.ShapeDtypeStruct((WIDE, SLOT, TILE), BF),
            jax.ShapeDtypeStruct((WIDE, 2 * SLOT, TILE), BF),
        ),
        in_specs=[smem, smem, hbm, hbm, hbm, vmem, vmem, vmem, hbm],
        out_specs=(hbm, hbm, hbm, hbm),
        scratch_shapes=[
            pltpu.VMEM((TILES, TILE, TILE), BF),
            pltpu.VMEM(((SRC + 1) * quads, SLOT, TILE), BF),
            pltpu.VMEM((DST * TILE, 2 * TILE), BF),
            pltpu.VMEM((DST * TILE, 2 * TILE), BF),
            pltpu.VMEM((DST, TILE, TILE), F32),
            pltpu.VMEM((WIDE, SLOT, TILE), BF),
            pltpu.VMEM((WIDE, 2 * SLOT, TILE), BF),
            pltpu.VMEM((DST + 1, TILE, TILE), F32),
            pltpu.VMEM((DST + 1, TILE, TILE), BF),
            pltpu.VMEM((SRC + 1, TILE, TILE), F32),
            pltpu.VMEM((2 * TILE, 2 * TILE), F32),
            pltpu.VMEM((8, 2 * TILE), F32),
            dma((CHUNKS,)),
            dma((8,)),
        ],
        compiler_params=pltpu.CompilerParams(vmem_limit_bytes=60 * 2**20),
    )(list_f, list_b, feat, got, cot, w2, wt2, bias, tiles)


def reduce_kernel(
    hub_rows, rows, bound, msg, own, gfeat, g_self, g_neigh, g_bias,
    acc, back, sums, near_out, near_in, part, whole,
    s_back, r_back, s_sum, r_sum, s_near, r_near, s_part, r_part, s_own, s_out,
):
    w = lax.axis_index("wide")
    n = lax.axis_index("narrow")
    barrier = pltpu.get_barrier_semaphore()

    def greet(o, c):
        pl.semaphore_signal(
            barrier, inc=1, device_id=(lax.rem(w + o, WIDE), n), device_id_type=MESH
        )
        return c

    lax.fori_loop(1, WIDE, greet, 0)
    for k in range(1, NARROW):
        pl.semaphore_signal(
            barrier, inc=1, device_id=(w, lax.rem(n + k, NARROW)), device_id_type=MESH
        )
    load = pltpu.make_async_copy(own, acc, s_own.at[0])
    load.start()
    mine_sum = pltpu.make_async_copy(msg.at[w], sums.at[w], s_own.at[1])
    mine_sum.start()
    mine_back = pltpu.make_async_copy(bound.at[w], back.at[w], s_own.at[2])
    mine_back.start()
    pl.semaphore_wait(barrier, WIDE - 1 + NARROW - 1)

    def wide_copy(o, src, dst, send, recv):
        return pltpu.make_async_remote_copy(
            src_ref=src,
            dst_ref=dst,
            send_sem=send.at[o],
            recv_sem=recv.at[o],
            device_id=(lax.rem(w + o, WIDE), n),
            device_id_type=MESH,
        )

    def sum_copy(o, slot):
        return wide_copy(o, msg.at[lax.rem(w + o, WIDE)], sums.at[slot], s_sum, r_sum)

    def back_copy(o, slot):
        return wide_copy(o, bound.at[lax.rem(w + o, WIDE)], back.at[slot], s_back, r_back)

    def part_copy(o, slot):
        return wide_copy(o, part, whole.at[slot], s_part, r_part)

    def near_copy(k, slot):
        peer = lax.rem(n + k, NARROW)
        return pltpu.make_async_remote_copy(
            src_ref=near_out.at[peer],
            dst_ref=near_in.at[slot],
            send_sem=s_near.at[k],
            recv_sem=r_near.at[k],
            device_id=(w, peer),
            device_id_type=MESH,
        )

    def from_wide(o):
        return lax.rem(w + WIDE - o, WIDE)

    def send_sum(o, c):
        sum_copy(o, w).start()
        return c

    def send_back(o, c):
        back_copy(o, w).start()
        return c

    def send_part(o, c):
        part_copy(o, w).start()
        return c

    lax.fori_loop(1, WIDE, send_sum, 0)
    lax.fori_loop(1, WIDE, send_back, 0)

    def wait_sum(o, c):
        sum_copy(o, from_wide(o)).wait_recv()
        return c

    lax.fori_loop(1, WIDE, wait_sum, 0)
    mine_sum.wait()

    def add_up(q, total):
        return total + sums[q].astype(F32)

    total = lax.fori_loop(0, WIDE, add_up, jnp.zeros((2 * SLOT, TILE), F32))
    for k in range(NARROW):
        near_out[k] = jnp.concatenate([total[HUB * k : HUB * (k + 1)], total[SLOT : SLOT + 24]], 0)
    near_in[n] = near_out[n]
    for k in range(1, NARROW):
        near_copy(k, n).start()

    def wait_back(o, c):
        back_copy(o, from_wide(o)).wait_recv()
        return c

    lax.fori_loop(1, WIDE, wait_back, 0)
    mine_back.wait()
    for k in range(1, NARROW):
        near_copy(k, lax.rem(n + NARROW - k, NARROW)).wait_recv()
    near = near_in[0] + near_in[1] + near_in[2] + near_in[3]
    part[...] = near[HUB : HUB + 16]
    whole[w] = near[HUB : HUB + 16]
    lax.fori_loop(1, WIDE, send_part, 0)
    g_bias[...] = jnp.concatenate([near[24:25], near[25:26]], axis=1)

    high = near[0:HUB].astype(BF)
    low = (near[0:HUB] - high.astype(F32)).astype(BF)
    values = jnp.concatenate(
        [
            back[...].reshape(WIDE * SLOT, TILE),
            jnp.concatenate([high, low], axis=0),
            jnp.zeros((TILE - 2 * HUB, TILE), BF),
        ],
        axis=0,
    )
    lane = iota((1, TILE), 1)
    hub_at = jnp.full((1, TILE), -1, I32)
    for j in range(HUB):
        hub_at = jnp.where((lane == j) | (lane == j + HUB), hub_rows[j], hub_at)
    where = jnp.concatenate(
        [rows[pl.ds(r, 1), :] for r in range(WIDE * SLOT // TILE)] + [hub_at], axis=1
    )
    load.wait()
    step = 512
    span = where.shape[1]

    def scatter(i, c):
        at = pl.ds(i * step, step)
        hot = jnp.where(iota((step, span), 0) + i * step == where, 1.0, 0.0).astype(BF)
        acc[at, :] += mm(hot, values)
        return c

    lax.fori_loop(0, DST * TILE // step, scatter, 0)
    store = pltpu.make_async_copy(acc, gfeat, s_out.at[0])
    store.start()

    def wait_part(o, c):
        part_copy(o, from_wide(o)).wait_recv()
        return c

    lax.fori_loop(1, WIDE, wait_part, 0)
    for out, first in ((g_self, 0), (g_neigh, WIDE // 2)):
        for p in range(WIDE // 2):
            out[pl.ds(8 * p, 8), :] = jnp.concatenate(
                [whole[first + p, pl.ds(0, 8), :], whole[first + p, pl.ds(8, 8), :]], axis=1
            )

    def sent(o, c):
        sum_copy(o, w).wait_send()
        back_copy(o, w).wait_send()
        part_copy(o, w).wait_send()
        return c

    lax.fori_loop(1, WIDE, sent, 0)
    for k in range(1, NARROW):
        near_copy(k, n).wait_send()
    store.wait()


def reduce(hub_rows, rows, bound, msg, own):
    smem = pl.BlockSpec(memory_space=pltpu.SMEM)
    vmem = pl.BlockSpec(memory_space=pltpu.VMEM)
    hbm = pl.BlockSpec(memory_space=pl.ANY)
    dma = pltpu.SemaphoreType.DMA
    return pl.pallas_call(
        reduce_kernel,
        out_shape=(
            jax.ShapeDtypeStruct((DST * TILE, TILE), F32),
            jax.ShapeDtypeStruct((TILE, 2 * TILE), F32),
            jax.ShapeDtypeStruct((TILE, 2 * TILE), F32),
            jax.ShapeDtypeStruct((1, 2 * TILE), F32),
        ),
        in_specs=[smem, vmem, hbm, hbm, hbm],
        out_specs=(hbm, vmem, vmem, vmem),
        scratch_shapes=[
            pltpu.VMEM((DST * TILE, TILE), F32),
            pltpu.VMEM((WIDE, SLOT, TILE), BF),
            pltpu.VMEM((WIDE, 2 * SLOT, TILE), BF),
            pltpu.VMEM((NARROW, 32, TILE), F32),
            pltpu.VMEM((NARROW, 32, TILE), F32),
            pltpu.VMEM((16, TILE), F32),
            pltpu.VMEM((WIDE, 16, TILE), F32),
            dma((WIDE,)), dma((WIDE,)), dma((WIDE,)), dma((WIDE,)),
            dma((NARROW,)), dma((NARROW,)), dma((WIDE,)), dma((WIDE,)),
            dma((3,)), dma((1,)),
        ],
        compiler_params=pltpu.CompilerParams(
            collective_id=1, has_side_effects=True, vmem_limit_bytes=32 * 2**20
        ),
    )(hub_rows, rows, bound, msg, own)


def on_device(
    features, cotangent, w_self, w_neigh, bias, tile_weights, tile_src, tile_dst, tile_live,
    send_rows, hub_rows,
):
    quads = TILE // SLOT
    lanes = (TILES // TILE, TILE)
    got, list_f, list_b = fetch(
        features, send_rows, hub_rows,
        tile_src.reshape(lanes), tile_dst.reshape(lanes), tile_live.reshape(lanes),
    )
    w2 = jnp.concatenate([w_self, w_neigh], axis=0)
    hidden, own, bound, msg = layer(
        list_f, list_b, features.reshape(DST * quads, SLOT, TILE), got, cotangent,
        w2, w2, bias.reshape(1, 2 * TILE), tile_weights,
    )
    grad_features, grad_self, grad_neigh, grad_bias = reduce(
        hub_rows, send_rows.reshape(WIDE * SLOT // TILE, TILE), bound, msg,
        own.reshape(DST * TILE, TILE),
    )
    return (hidden, grad_features, grad_self, grad_neigh, grad_bias.reshape(2 * TILE))


def solution(mesh):
    both = ("wide", "narrow")
    placed = (
        P(both, None), P(both, None), P(), P(), P(), P(both, None, None),
        P(both), P(both), P(both), P(both, None), P(both),
    )
    return jax.shard_map(
        on_device,
        mesh=mesh,
        in_specs=placed,
        out_specs=(P(both, None), P(both, None), P(), P(), P()),
        check_vma=False,
    )
```

```python
import functools

import jax
import jax.numpy as jnp
from jax import lax
from jax.experimental import pallas as pl
from jax.experimental.pallas import tpu as pltpu
from jax.sharding import PartitionSpec as P

MESH = pl.DeviceIdType.MESH
BF, F32, I32 = jnp.bfloat16, jnp.float32, jnp.int32
TILE = 128
DST = 32
SRC = 48
TILES = 512
SLOTS = 640
UNROLL = 16
ROWS = 1024
CHUNKS = 8
SLOT = 32
QUADS = TILE // SLOT
HUB = 8
WIDE = 32
NARROW = 4
GELU_A = 0.7978845608028654
GELU_B = 0.044715


def mm(a, b):
    return jnp.dot(a, b, preferred_element_type=F32)


def nt(a, b):
    return lax.dot_general(a, b, (((1,), (1,)), ((), ())), preferred_element_type=F32)


def tn(a, b):
    return lax.dot_general(a, b, (((0,), (0,)), ((), ())), preferred_element_type=F32)


def iota(shape, dim):
    return lax.broadcasted_iota(I32, shape, dim)


def tile_list(key, other, live, keys, zero):
    groups = 64
    hot = jnp.where((iota((groups, TILES), 0) == key) & (live > 0), 1.0, 0.0)
    before = jnp.where(iota((TILES, TILES), 0) < iota((TILES, TILES), 1), 1.0, 0.0).astype(BF)
    rank = mm(hot.astype(BF), before)
    count = jnp.sum(hot, axis=1, keepdims=True).astype(I32)
    even = ((count + 1) // 2 * 2).astype(F32)
    lower = jnp.where(iota((groups, groups), 1) < iota((groups, groups), 0), 1.0, 0.0).astype(BF)
    start = mm(lower, jnp.broadcast_to(even, (groups, TILE)).astype(BF))[:, :1]
    total = jnp.sum(even, axis=0, keepdims=True)
    place = jnp.sum(hot * (rank + start), axis=0, keepdims=True).astype(I32)
    place = jnp.where(live > 0, place, -1)
    at = jnp.where(iota((SLOTS, TILES), 0) == place, 1.0, 0.0).astype(BF)
    t = iota((1, TILES), 1)
    rows = [t // 16, t % 16, other - zero, key - keys]
    row = iota((8, TILES), 0)
    values = jnp.zeros((8, TILES), I32)
    for r, v in enumerate(rows):
        values = jnp.where(row == r, v, values)
    got = nt(values.astype(F32).astype(BF), at).astype(I32)
    pairs = (total * 0.5).astype(I32)
    out = jnp.concatenate(
        [
            got[0:1] * 16 + got[1:2],
            got[2:3] + zero,
            got[3:4] + keys,
            jnp.broadcast_to(pairs, (1, SLOTS)),
        ],
        axis=0,
    )
    return out


def greet_all(w, n):
    barrier = pltpu.get_barrier_semaphore()

    def greet(o, c):
        pl.semaphore_signal(
            barrier, inc=1, device_id=(lax.rem(w + o, WIDE), n), device_id_type=MESH
        )
        return c

    lax.fori_loop(1, WIDE, greet, 0)
    for k in range(1, NARROW):
        pl.semaphore_signal(
            barrier, inc=1, device_id=(w, lax.rem(n + k, NARROW)), device_id_type=MESH
        )
    return barrier


def fetch_kernel(
    feat, cot, w_self, w_neigh, bias, tiles, src, dst, live, send_rows, hub_rows,
    wbuf, buf, cotb, w2, b2, list_f, list_b,
    send_at, hub_at, keys, wide32, hubs, picked, msg, near, own, lists,
    s_row, r_row, s_hub, r_hub, s_near, r_near, s_own, s_in, s_big, s_list,
):
    w = lax.axis_index("wide")
    n = lax.axis_index("narrow")
    small = [
        pltpu.make_async_copy(send_rows, send_at, s_in.at[0]),
        pltpu.make_async_copy(hub_rows, hub_at, s_in.at[1]),
        pltpu.make_async_copy(feat, buf.at[pl.ds(0, DST * QUADS)], s_in.at[2]),
        pltpu.make_async_copy(src, keys.at[0], s_in.at[3]),
        pltpu.make_async_copy(dst, keys.at[1], s_in.at[4]),
        pltpu.make_async_copy(live, keys.at[2], s_in.at[5]),
    ]
    for c in small:
        c.start()
    barrier = greet_all(w, n)
    big = [
        pltpu.make_async_copy(w_self, w2.at[pl.ds(0, TILE)], s_big.at[0]),
        pltpu.make_async_copy(w_neigh, w2.at[pl.ds(TILE, TILE)], s_big.at[1]),
        pltpu.make_async_copy(bias, b2, s_big.at[2]),
        pltpu.make_async_copy(cot, cotb, s_big.at[3]),
    ]
    per = TILES // CHUNKS
    big += [
        pltpu.make_async_copy(
            tiles.at[pl.ds(i * per, per)], wbuf.at[pl.ds(i * per, per)], s_big.at[4 + i]
        )
        for i in range(CHUNKS)
    ]
    for c in big:
        c.start()
    buf[pl.ds(SRC * QUADS, QUADS)] = jnp.zeros((QUADS, SLOT, TILE), BF)
    for c in small[:3]:
        c.wait()
    wide32[...] = buf[pl.ds(0, DST * QUADS)].astype(F32).reshape(DST * TILE, TILE)
    for j in range(HUB):
        hubs[pl.ds(j, 1), :] = wide32[pl.ds(hub_at[j], 1), :]

    def pick(p, c):
        for j in range(SLOT):
            picked[pl.ds(p * SLOT + j, 1), :] = wide32[pl.ds(send_at[p, j], 1), :]
        return c

    lax.fori_loop(0, WIDE, pick, 0)
    msg[...] = picked[...].astype(BF).reshape(WIDE, SLOT, TILE)
    near[n] = hubs[...]

    pl.semaphore_wait(barrier, WIDE - 1 + NARROW - 1)
    rows_at, hubs_at = DST * QUADS, DST * QUADS + WIDE

    def near_copy(k, slot):
        return pltpu.make_async_remote_copy(
            src_ref=hubs,
            dst_ref=near.at[slot],
            send_sem=s_near.at[k],
            recv_sem=r_near.at[k],
            device_id=(w, lax.rem(n + k, NARROW)),
            device_id_type=MESH,
        )

    def row_copy(o, slot):
        p = lax.rem(w + o, WIDE)
        return pltpu.make_async_remote_copy(
            src_ref=msg.at[p],
            dst_ref=buf.at[rows_at + slot],
            send_sem=s_row.at[o],
            recv_sem=r_row.at[o],
            device_id=(p, n),
            device_id_type=MESH,
        )

    def hub_copy(o, slot):
        return pltpu.make_async_remote_copy(
            src_ref=own,
            dst_ref=buf.at[hubs_at + slot],
            send_sem=s_hub.at[o],
            recv_sem=r_hub.at[o],
            device_id=(lax.rem(w + o, WIDE), n),
            device_id_type=MESH,
        )

    for k in range(1, NARROW):
        near_copy(k, n).start()

    def send_row(o, c):
        row_copy(o, w).start()
        return c

    lax.fori_loop(1, WIDE, send_row, 0)
    mine_row = pltpu.make_async_copy(msg.at[w], buf.at[rows_at + w], s_own.at[0])
    mine_row.start()
    for k in range(1, NARROW):
        near_copy(k, lax.rem(n + NARROW - k, NARROW)).wait_recv()
    own[...] = near[...].reshape(NARROW * HUB, TILE).astype(BF)

    def send_hub(o, c):
        hub_copy(o, w).start()
        return c

    lax.fori_loop(1, WIDE, send_hub, 0)
    mine_hub = pltpu.make_async_copy(own, buf.at[hubs_at + w], s_own.at[1])
    mine_hub.start()

    for c in small[3:]:
        c.wait()

    def flat(i):
        return jnp.concatenate([keys[i, pl.ds(r, 1), :] for r in range(TILES // TILE)], axis=1)

    s, d, l = flat(0), flat(1), flat(2)
    lists[0] = tile_list(d, s, l, DST, SRC)
    lists[1] = tile_list(s, d, l, SRC, DST)
    out_lists = [
        pltpu.make_async_copy(lists.at[0], list_f, s_list.at[0]),
        pltpu.make_async_copy(lists.at[1], list_b, s_list.at[1]),
    ]
    for c in out_lists:
        c.start()

    def finish(o, c):
        slot = lax.rem(w + WIDE - o, WIDE)
        row_copy(o, slot).wait()
        hub_copy(o, slot).wait()
        return c

    lax.fori_loop(1, WIDE, finish, 0)
    for k in range(1, NARROW):
        near_copy(k, n).wait_send()
    mine_row.wait()
    mine_hub.wait()
    for c in out_lists:
        c.wait()
    for c in big:
        c.wait()


def in_vmem(x):
    return pltpu.with_memory_space_constraint(x, pltpu.VMEM)


def in_hbm(x):
    return pltpu.with_memory_space_constraint(x, pltpu.HBM)


def fetch(feat, cot, w_self, w_neigh, bias, tiles, src, dst, live, send_rows, hub_rows):
    vmem = pl.BlockSpec(memory_space=pltpu.VMEM)
    hbm = pl.BlockSpec(memory_space=pltpu.HBM)
    dma = pltpu.SemaphoreType.DMA
    return pl.pallas_call(
        fetch_kernel,
        out_shape=(
            pltpu.VMEM((TILES, TILE, TILE), BF),
            pltpu.VMEM(((SRC + 1) * QUADS, SLOT, TILE), BF),
            pltpu.VMEM((DST * TILE, 2 * TILE), BF),
            pltpu.VMEM((2 * TILE, 2 * TILE), BF),
            pltpu.VMEM((1, 2 * TILE), F32),
            pltpu.HBM((4, SLOTS), I32),
            pltpu.HBM((4, SLOTS), I32),
        ),
        in_specs=[hbm] * 11,
        out_specs=(vmem, vmem, vmem, vmem, vmem, hbm, hbm),
        scratch_shapes=[
            pltpu.SMEM((WIDE, SLOT), I32),
            pltpu.SMEM((HUB,), I32),
            pltpu.VMEM((3, TILES // TILE, TILE), I32),
            pltpu.VMEM((DST * TILE, TILE), F32),
            pltpu.VMEM((HUB, TILE), F32),
            pltpu.VMEM((WIDE * SLOT, TILE), F32),
            pltpu.VMEM((WIDE, SLOT, TILE), BF),
            pltpu.VMEM((NARROW, HUB, TILE), F32),
            pltpu.VMEM((NARROW * HUB, TILE), BF),
            pltpu.VMEM((2, 4, SLOTS), I32),
            dma((WIDE,)), dma((WIDE,)), dma((WIDE,)), dma((WIDE,)),
            dma((NARROW,)), dma((NARROW,)), dma((2,)), dma((6,)), dma((4 + CHUNKS,)), dma((2,)),
        ],
        compiler_params=pltpu.CompilerParams(
            collective_id=0, has_side_effects=True, vmem_limit_bytes=30 * 2**20
        ),
    )(
        *map(in_hbm, (feat, cot, w_self, w_neigh, bias, tiles, src, dst, live, send_rows, hub_rows))
    )


def layer_kernel(
    lists_f, lists_b, wbuf, buf, cotb, w2, bias, hidden, own, bound, sums, hubs,
    list_f, list_b, hidb, agg, gt, gbt, wg, gb, sem,
):
    loads = [
        pltpu.make_async_copy(lists_f, list_f, sem.at[0]),
        pltpu.make_async_copy(lists_b, list_b, sem.at[1]),
    ]
    for c in loads:
        c.start()

    def clear(i, c):
        agg[i] = jnp.zeros((TILE, TILE), F32)
        return c

    lax.fori_loop(0, DST + 1, clear, 0)

    def clear_back(i, c):
        gbt[DST + i] = jnp.zeros((TILE, TILE), F32)
        return c

    lax.fori_loop(0, SRC - DST + 1, clear_back, 0)
    gt[DST] = jnp.zeros((TILE, TILE), BF)
    gb[...] = jnp.zeros_like(gb)
    wg[...] = jnp.zeros_like(wg)
    for c in loads:
        c.wait()

    def rows_of(s):
        return buf[pl.ds(s * QUADS, QUADS)].reshape(TILE, TILE)

    def forward(i, c):
        parts = []
        for u in range(UNROLL):
            k = 2 * (i * UNROLL + u)
            left = jnp.concatenate([wbuf[list_f[0, k]], wbuf[list_f[0, k + 1]]], axis=1)
            right = jnp.concatenate(
                [rows_of(list_f[1, k]), rows_of(list_f[1, k + 1])], axis=0
            )
            parts.append(mm(left, right))
        for u in range(UNROLL):
            agg[list_f[2, 2 * (i * UNROLL + u)]] += parts[u]
        return c

    lax.fori_loop(0, (list_f[3, 0] + UNROLL - 1) // UNROLL, forward, 0)
    blocks = ROWS // TILE

    def dense(i, c):
        rows = pl.ds(i * ROWS, ROWS)
        f = buf[pl.ds(i * blocks * QUADS, blocks * QUADS)].reshape(ROWS, TILE)
        a = agg[pl.ds(i * blocks, blocks)].reshape(ROWS, TILE).astype(BF)
        x = jnp.concatenate([f, a], axis=1)
        pre = mm(x, w2[...]) + bias[...]
        square = pre * pre
        t = jnp.tanh(pre * (GELU_A + (GELU_A * GELU_B) * square))
        half = 0.5 + 0.5 * t
        hidb[rows, :] = (pre * half).astype(BF)
        slope = half + pre * (0.5 - 0.5 * t * t) * (GELU_A + (3 * GELU_A * GELU_B) * square)
        gp = (cotb[rows, :].astype(F32) * slope).astype(BF)
        wg[...] += tn(x, gp)
        gb[...] += jnp.sum(gp.astype(F32).reshape(ROWS // 8, 8, 2 * TILE), axis=0)
        g2 = nt(w2[...], gp)
        for j in range(blocks):
            gbt[i * blocks + j] = g2[:TILE, j * TILE : (j + 1) * TILE]
            gt[i * blocks + j] = g2[TILE:, j * TILE : (j + 1) * TILE].astype(BF)
        return c

    lax.fori_loop(0, DST // blocks, dense, 0)
    out_hidden = pltpu.make_async_copy(hidb, hidden, sem.at[2])
    out_hidden.start()

    def backward(i, c):
        parts = []
        for u in range(UNROLL):
            k = 2 * (i * UNROLL + u)
            left = jnp.concatenate([gt[list_b[1, k]], gt[list_b[1, k + 1]]], axis=1)
            right = jnp.concatenate([wbuf[list_b[0, k]], wbuf[list_b[0, k + 1]]], axis=0)
            parts.append(mm(left, right))
        for u in range(UNROLL):
            gbt[list_b[2, 2 * (i * UNROLL + u)]] += parts[u]
        return c

    lax.fori_loop(0, (list_b[3, 0] + UNROLL - 1) // UNROLL, backward, 0)

    def finish_own(i, c):
        own[pl.ds(i * TILE, TILE), :] = gbt[i].T
        return c

    lax.fori_loop(0, DST, finish_own, 0, unroll=4)
    bias_sum = jnp.sum(gb[...], axis=0, keepdims=True)
    row = iota((16, TILE), 0)
    bias_rows = jnp.where(
        row == 0, bias_sum[:, :TILE], jnp.where(row == 1, bias_sum[:, TILE:], 0.0)
    ).astype(BF)
    for i in range(WIDE // QUADS):
        at = pl.ds(i * QUADS, QUADS)
        bound[at] = gbt[DST + i].T.astype(BF).reshape(QUADS, SLOT, TILE)
        hubs[at] = gbt[DST + WIDE // QUADS + i].T.astype(BF).reshape(QUADS, SLOT, TILE)
    for p in range(WIDE):
        part = wg[pl.ds(8 * p, 8), :]
        sums[p, pl.ds(0, 16), :] = jnp.concatenate(
            [part[:, :TILE], part[:, TILE:]], axis=0
        ).astype(BF)
        sums[p, pl.ds(16, 16), :] = bias_rows
    out_hidden.wait()


def layer(list_f, list_b, wbuf, buf, cotb, w2, bias):
    vmem = pl.BlockSpec(memory_space=pltpu.VMEM)
    hbm = pl.BlockSpec(memory_space=pltpu.HBM)
    return pl.pallas_call(
        layer_kernel,
        out_shape=(
            jax.ShapeDtypeStruct((DST * TILE, 2 * TILE), BF),
            pltpu.VMEM((DST * TILE, TILE), F32),
            pltpu.VMEM((WIDE, SLOT, TILE), BF),
            pltpu.VMEM((WIDE, SLOT, TILE), BF),
            pltpu.VMEM((WIDE, SLOT, TILE), BF),
        ),
        in_specs=[hbm, hbm, vmem, vmem, vmem, vmem, vmem],
        out_specs=(hbm, vmem, vmem, vmem, vmem),
        scratch_shapes=[
            pltpu.SMEM((4, SLOTS), I32),
            pltpu.SMEM((4, SLOTS), I32),
            pltpu.VMEM((DST * TILE, 2 * TILE), BF),
            pltpu.VMEM((DST + 1, TILE, TILE), F32),
            pltpu.VMEM((DST + 1, TILE, TILE), BF),
            pltpu.VMEM((SRC + 1, TILE, TILE), F32),
            pltpu.VMEM((2 * TILE, 2 * TILE), F32),
            pltpu.VMEM((8, 2 * TILE), F32),
            pltpu.SemaphoreType.DMA((3,)),
        ],
        compiler_params=pltpu.CompilerParams(vmem_limit_bytes=30 * 2**20),
    )(
        in_hbm(list_f), in_hbm(list_b),
        in_vmem(wbuf), in_vmem(buf), in_vmem(cotb), in_vmem(w2), in_vmem(bias),
    )


def reduce_kernel(
    hub_rows, send_rows, own, bound, sums, hubs, acc, whole, total_bias,
    hub_at, send_at, hot, back, sum_in, hub_in, sum_out, sum_near, hub_out, hub_near, part,
    s_back, r_back, s_sum, r_sum, s_hub, r_hub, s_part, r_part,
    s_sum_near, r_sum_near, s_hub_near, r_hub_near, s_in,
):
    w = lax.axis_index("wide")
    n = lax.axis_index("narrow")
    loads = [
        pltpu.make_async_copy(hub_rows, hub_at, s_in.at[0]),
        pltpu.make_async_copy(send_rows, send_at, s_in.at[1]),
    ]
    for c in loads:
        c.start()
    barrier = greet_all(w, n)
    pl.semaphore_wait(barrier, WIDE - 1 + NARROW - 1)

    def wide_copy(o, src, dst, send, recv):
        return pltpu.make_async_remote_copy(
            src_ref=src,
            dst_ref=dst,
            send_sem=send.at[o],
            recv_sem=recv.at[o],
            device_id=(lax.rem(w + o, WIDE), n),
            device_id_type=MESH,
        )

    def near_copy(k, src, dst, send, recv):
        return pltpu.make_async_remote_copy(
            src_ref=src,
            dst_ref=dst,
            send_sem=send.at[k],
            recv_sem=recv.at[k],
            device_id=(w, lax.rem(n + k, NARROW)),
            device_id_type=MESH,
        )

    def sum_copy(o, slot):
        return wide_copy(o, sums.at[lax.rem(w + o, WIDE)], sum_in.at[slot], s_sum, r_sum)

    def hub_copy(o, slot):
        return wide_copy(o, hubs.at[lax.rem(w + o, WIDE)], hub_in.at[slot], s_hub, r_hub)

    def back_copy(o, slot):
        return wide_copy(o, bound.at[lax.rem(w + o, WIDE)], back.at[slot], s_back, r_back)

    def part_copy(o, slot):
        return wide_copy(o, part, whole.at[slot], s_part, r_part)

    def sum_near_copy(k, slot):
        return near_copy(k, sum_out, sum_near.at[slot], s_sum_near, r_sum_near)

    def hub_near_copy(k, slot):
        peer = lax.rem(n + k, NARROW)
        return near_copy(k, hub_out.at[peer], hub_near.at[slot], s_hub_near, r_hub_near)

    def send(copy):
        def one(o, c):
            copy(o, w).start()
            return c

        lax.fori_loop(1, WIDE, one, 0)

    def arrive(copy):
        def one(o, c):
            copy(o, lax.rem(w + WIDE - o, WIDE)).wait_recv()
            return c

        lax.fori_loop(1, WIDE, one, 0)

    def near_arrive(copy):
        for k in range(1, NARROW):
            copy(k, lax.rem(n + NARROW - k, NARROW)).wait_recv()

    send(sum_copy)
    send(hub_copy)
    send(back_copy)
    sum_in[w] = sums[w]
    hub_in[w] = hubs[w]
    back[w] = bound[w]

    for c in loads:
        c.wait()
    lane = iota((1, TILE), 1)
    hub_lane = jnp.full((1, TILE), -1, I32)
    for j in range(HUB):
        hub_lane = jnp.where((lane == j) | (lane == j + HUB), hub_at[j], hub_lane)
    where = jnp.concatenate(
        [send_at[pl.ds(p, 1), :] for p in range(WIDE)] + [hub_lane], axis=1
    )
    step, span = 512, WIDE * SLOT + TILE

    def mark(i, c):
        hit = iota((step, span), 0) + i * step == where
        hot[pl.ds(i * step, step), :] = jnp.where(hit, 1.0, 0.0).astype(BF)
        return c

    lax.fori_loop(0, DST * TILE // step, mark, 0)

    def add_up(ref, rows):
        def one(q, total):
            return total + ref[q].astype(F32)

        return lax.fori_loop(0, WIDE, one, jnp.zeros((rows, TILE), F32))

    arrive(sum_copy)
    sum_out[...] = add_up(sum_in, SLOT)[:24]
    sum_near[n] = sum_out[...]
    for k in range(1, NARROW):
        sum_near_copy(k, n).start()
    arrive(hub_copy)
    hub_sum = add_up(hub_in, SLOT)
    for k in range(NARROW):
        hub_out[k] = hub_sum[HUB * k : HUB * (k + 1)]
    hub_near[n] = hub_out[n]
    for k in range(1, NARROW):
        hub_near_copy(k, n).start()
    near_arrive(sum_near_copy)
    near = sum_near[0] + sum_near[1] + sum_near[2] + sum_near[3]
    part[...] = near[0:16].astype(BF)
    whole[w] = near[0:16].astype(BF)
    send(part_copy)
    total_bias[...] = near[16:24]

    near_arrive(hub_near_copy)
    mine = hub_near[0] + hub_near[1] + hub_near[2] + hub_near[3]
    high = mine.astype(BF)
    low = (mine - high.astype(F32)).astype(BF)
    arrive(back_copy)
    values = jnp.concatenate(
        [
            back[...].reshape(WIDE * SLOT, TILE),
            jnp.concatenate([high, low], axis=0),
            jnp.zeros((TILE - 2 * HUB, TILE), BF),
        ],
        axis=0,
    )

    def scatter(i, c):
        at = pl.ds(i * step, step)
        acc[at, :] = own[at, :] + mm(hot[at, :], values)
        return c

    lax.fori_loop(0, DST * TILE // step, scatter, 0)
    arrive(part_copy)

    def sent(o, c):
        sum_copy(o, w).wait_send()
        hub_copy(o, w).wait_send()
        back_copy(o, w).wait_send()
        part_copy(o, w).wait_send()
        return c

    lax.fori_loop(1, WIDE, sent, 0)
    for k in range(1, NARROW):
        sum_near_copy(k, n).wait_send()
        hub_near_copy(k, n).wait_send()


def reduce(hub_rows, send_rows, own, bound, sums, hubs):
    vmem = pl.BlockSpec(memory_space=pltpu.VMEM)
    hbm = pl.BlockSpec(memory_space=pltpu.HBM)
    dma = pltpu.SemaphoreType.DMA
    return pl.pallas_call(
        reduce_kernel,
        out_shape=(
            pltpu.VMEM((DST * TILE, TILE), F32),
            pltpu.VMEM((WIDE, 16, TILE), BF),
            pltpu.VMEM((8, TILE), F32),
        ),
        in_specs=[hbm, hbm, vmem, vmem, vmem, vmem],
        out_specs=(vmem, vmem, vmem),
        scratch_shapes=[
            pltpu.SMEM((HUB,), I32),
            pltpu.VMEM((WIDE, SLOT), I32),
            pltpu.VMEM((DST * TILE, WIDE * SLOT + TILE), BF),
            pltpu.VMEM((WIDE, SLOT, TILE), BF),
            pltpu.VMEM((WIDE, SLOT, TILE), BF),
            pltpu.VMEM((WIDE, SLOT, TILE), BF),
            pltpu.VMEM((24, TILE), F32),
            pltpu.VMEM((NARROW, 24, TILE), F32),
            pltpu.VMEM((NARROW, HUB, TILE), F32),
            pltpu.VMEM((NARROW, HUB, TILE), F32),
            pltpu.VMEM((16, TILE), BF),
            dma((WIDE,)), dma((WIDE,)), dma((WIDE,)), dma((WIDE,)),
            dma((WIDE,)), dma((WIDE,)), dma((WIDE,)), dma((WIDE,)),
            dma((NARROW,)), dma((NARROW,)), dma((NARROW,)), dma((NARROW,)), dma((2,)),
        ],
        compiler_params=pltpu.CompilerParams(
            collective_id=1, has_side_effects=True, vmem_limit_bytes=30 * 2**20
        ),
    )(
        in_hbm(hub_rows), in_hbm(send_rows),
        in_vmem(own), in_vmem(bound), in_vmem(sums), in_vmem(hubs),
    )


def finish_kernel(acc, whole, total_bias, gfeat, g_self, g_neigh, g_bias, weights, bias, sem):
    store = pltpu.make_async_copy(acc, gfeat, sem.at[0])
    store.start()
    for p in range(WIDE):
        got = whole[p].astype(F32)
        weights[pl.ds(8 * p, 8), :] = jnp.concatenate([got[:8], got[8:]], axis=1)
    bias[...] = jnp.concatenate([total_bias[pl.ds(0, 1), :], total_bias[pl.ds(1, 1), :]], axis=1)
    outs = [
        pltpu.make_async_copy(weights.at[pl.ds(0, TILE)], g_self, sem.at[1]),
        pltpu.make_async_copy(weights.at[pl.ds(TILE, TILE)], g_neigh, sem.at[2]),
        pltpu.make_async_copy(bias, g_bias, sem.at[3]),
    ]
    for c in outs:
        c.start()
    store.wait()
    for c in outs:
        c.wait()


def finish(acc, whole, total_bias):
    vmem = pl.BlockSpec(memory_space=pltpu.VMEM)
    hbm = pl.BlockSpec(memory_space=pltpu.HBM)
    return pl.pallas_call(
        finish_kernel,
        out_shape=(
            jax.ShapeDtypeStruct((DST * TILE, TILE), F32),
            jax.ShapeDtypeStruct((TILE, 2 * TILE), F32),
            jax.ShapeDtypeStruct((TILE, 2 * TILE), F32),
            jax.ShapeDtypeStruct((1, 2 * TILE), F32),
        ),
        in_specs=[vmem, vmem, vmem],
        out_specs=(hbm, hbm, hbm, hbm),
        scratch_shapes=[
            pltpu.VMEM((2 * TILE, 2 * TILE), F32),
            pltpu.VMEM((1, 2 * TILE), F32),
            pltpu.SemaphoreType.DMA((4,)),
        ],
    )(in_vmem(acc), in_vmem(whole), in_vmem(total_bias))


def on_device(
    features, cotangent, w_self, w_neigh, bias, tile_weights, tile_src, tile_dst, tile_live,
    send_rows, hub_rows,
):
    lanes = (TILES // TILE, TILE)
    wbuf, buf, cotb, w2, b2, list_f, list_b = fetch(
        features.reshape(DST * QUADS, SLOT, TILE), cotangent, w_self, w_neigh,
        bias.reshape(1, 2 * TILE), tile_weights,
        tile_src.reshape(lanes), tile_dst.reshape(lanes), tile_live.reshape(lanes),
        send_rows, hub_rows,
    )
    hidden, own, bound, sums, hubs = layer(list_f, list_b, wbuf, buf, cotb, w2, b2)
    acc, whole, total_bias = reduce(hub_rows, send_rows, own, bound, sums, hubs)
    grad_features, grad_self, grad_neigh, grad_bias = finish(acc, whole, total_bias)
    return (hidden, grad_features, grad_self, grad_neigh, grad_bias.reshape(2 * TILE))


def solution(mesh):
    both = ("wide", "narrow")
    placed = (
        P(both, None), P(both, None), P(), P(), P(), P(both, None, None),
        P(both), P(both), P(both), P(both, None), P(both),
    )
    return jax.shard_map(
        on_device,
        mesh=mesh,
        in_specs=placed,
        out_specs=(P(both, None), P(both, None), P(), P(), P()),
        check_vma=False,
    )
```

```python
import functools

import jax
import jax.numpy as jnp
from jax import lax
from jax.experimental import pallas as pl
from jax.experimental.pallas import tpu as pltpu
from jax.sharding import PartitionSpec as P

MESH = pl.DeviceIdType.MESH
BF, F32, I32 = jnp.bfloat16, jnp.float32, jnp.int32
TILE = 128
DST = 32
SRC = 48
TILES = 512
SLOTS = 640
UNROLL = 16
PAIRS = 288
COUNT = 64
ROWS = 1024
CHUNKS = 8
VMEM_LIMIT = 32 * 2**20
SLOT = 32
QUADS = TILE // SLOT
HUB = 8
WIDE = 32
NARROW = 4
GELU_A = 0.7978845608028654
GELU_B = 0.044715


def mm(a, b):
    return jnp.dot(a, b, preferred_element_type=F32)


def nt(a, b):
    return lax.dot_general(a, b, (((1,), (1,)), ((), ())), preferred_element_type=F32)


def tn(a, b):
    return lax.dot_general(a, b, (((0,), (0,)), ((), ())), preferred_element_type=F32)


def iota(shape, dim):
    return lax.broadcasted_iota(I32, shape, dim)


def tile_list(key, other, live, keys, zero):
    groups = 64
    hot = jnp.where((iota((groups, TILES), 0) == key) & (live > 0), 1.0, 0.0)
    before = jnp.where(iota((TILES, TILES), 0) < iota((TILES, TILES), 1), 1.0, 0.0).astype(BF)
    rank = mm(hot.astype(BF), before)
    count = jnp.sum(hot, axis=1, keepdims=True).astype(I32)
    even = ((count + 1) // 2 * 2).astype(F32)
    lower = jnp.where(iota((groups, groups), 1) < iota((groups, groups), 0), 1.0, 0.0).astype(BF)
    start = mm(lower, jnp.broadcast_to(even, (groups, TILE)).astype(BF))[:, :1]
    total = jnp.sum(even, axis=0, keepdims=True)
    place = jnp.sum(hot * (rank + start), axis=0, keepdims=True).astype(I32)
    place = jnp.where(live > 0, place, -1)
    at = jnp.where(iota((SLOTS, TILES), 0) == place, 1.0, 0.0).astype(BF)
    t = iota((1, TILES), 1)
    rows = [t // 16, t % 16, other - zero, key - keys]
    row = iota((8, TILES), 0)
    values = jnp.zeros((8, TILES), I32)
    for r, v in enumerate(rows):
        values = jnp.where(row == r, v, values)
    got = nt(values.astype(F32).astype(BF), at).astype(I32)
    last = jnp.where(even > 0, (start + even) * 0.5 - 1.0, float(PAIRS))
    across = iota((groups, TILE), 0) == iota((groups, TILE), 1)
    last = jnp.sum(jnp.where(across, last, 0.0), axis=0, keepdims=True)
    info = jnp.where(iota((1, TILE), 1) < groups, last, total * 0.5).astype(I32)
    return jnp.concatenate(
        [
            got[0:1] * 16 + got[1:2],
            got[2:3] + zero,
            got[3:4] + keys,
            jnp.concatenate([info, jnp.zeros((1, SLOTS - TILE), I32)], axis=1),
        ],
        axis=0,
    )


def greet_all(w, n):
    barrier = pltpu.get_barrier_semaphore()

    def greet(o, c):
        pl.semaphore_signal(
            barrier, inc=1, device_id=(lax.rem(w + o, WIDE), n), device_id_type=MESH
        )
        return c

    lax.fori_loop(1, WIDE, greet, 0)
    for k in range(1, NARROW):
        pl.semaphore_signal(
            barrier, inc=1, device_id=(w, lax.rem(n + k, NARROW)), device_id_type=MESH
        )
    return barrier


def fetch_kernel(
    feat, cot, w_self, w_neigh, bias, tiles, src, dst, live, send_rows, hub_rows,
    wbuf, buf, cotb, w2, b2, list_f, list_b,
    send_at, hub_at, keys, wide32, hubs, picked, msg, near, own, lists,
    s_row, r_row, s_hub, r_hub, s_near, r_near, s_own, s_in, s_big, s_list,
):
    w = lax.axis_index("wide")
    n = lax.axis_index("narrow")
    small = [
        pltpu.make_async_copy(send_rows, send_at, s_in.at[0]),
        pltpu.make_async_copy(hub_rows, hub_at, s_in.at[1]),
        pltpu.make_async_copy(feat, buf.at[pl.ds(0, DST * QUADS)], s_in.at[2]),
        pltpu.make_async_copy(src, keys.at[0], s_in.at[3]),
        pltpu.make_async_copy(dst, keys.at[1], s_in.at[4]),
        pltpu.make_async_copy(live, keys.at[2], s_in.at[5]),
    ]
    for c in small:
        c.start()
    barrier = greet_all(w, n)
    big = [
        pltpu.make_async_copy(w_self, w2.at[pl.ds(0, TILE)], s_big.at[0]),
        pltpu.make_async_copy(w_neigh, w2.at[pl.ds(TILE, TILE)], s_big.at[1]),
        pltpu.make_async_copy(bias, b2, s_big.at[2]),
        pltpu.make_async_copy(cot, cotb, s_big.at[3]),
    ]
    per = TILES // CHUNKS
    big += [
        pltpu.make_async_copy(
            tiles.at[pl.ds(i * per, per)], wbuf.at[pl.ds(i * per, per)], s_big.at[4 + i]
        )
        for i in range(CHUNKS)
    ]
    for c in big:
        c.start()
    buf[pl.ds(SRC * QUADS, QUADS)] = jnp.zeros((QUADS, SLOT, TILE), BF)
    for c in small[:3]:
        c.wait()
    wide32[...] = buf[pl.ds(0, DST * QUADS)].astype(F32).reshape(DST * TILE, TILE)
    for j in range(HUB):
        hubs[pl.ds(j, 1), :] = wide32[pl.ds(hub_at[j], 1), :]

    def pick(p, c):
        for j in range(SLOT):
            picked[pl.ds(p * SLOT + j, 1), :] = wide32[pl.ds(send_at[p, j], 1), :]
        return c

    lax.fori_loop(0, WIDE, pick, 0)
    msg[...] = picked[...].astype(BF).reshape(WIDE, SLOT, TILE)
    near[n] = hubs[...]

    pl.semaphore_wait(barrier, WIDE - 1 + NARROW - 1)
    rows_at, hubs_at = DST * QUADS, DST * QUADS + WIDE

    def near_copy(k, slot):
        return pltpu.make_async_remote_copy(
            src_ref=hubs,
            dst_ref=near.at[slot],
            send_sem=s_near.at[k],
            recv_sem=r_near.at[k],
            device_id=(w, lax.rem(n + k, NARROW)),
            device_id_type=MESH,
        )

    def row_copy(o, slot):
        p = lax.rem(w + o, WIDE)
        return pltpu.make_async_remote_copy(
            src_ref=msg.at[p],
            dst_ref=buf.at[rows_at + slot],
            send_sem=s_row.at[o],
            recv_sem=r_row.at[o],
            device_id=(p, n),
            device_id_type=MESH,
        )

    def hub_copy(o, slot):
        return pltpu.make_async_remote_copy(
            src_ref=own,
            dst_ref=buf.at[hubs_at + slot],
            send_sem=s_hub.at[o],
            recv_sem=r_hub.at[o],
            device_id=(lax.rem(w + o, WIDE), n),
            device_id_type=MESH,
        )

    for k in range(1, NARROW):
        near_copy(k, n).start()

    def send_row(o, c):
        row_copy(o, w).start()
        return c

    lax.fori_loop(1, WIDE, send_row, 0)
    mine_row = pltpu.make_async_copy(msg.at[w], buf.at[rows_at + w], s_own.at[0])
    mine_row.start()
    for k in range(1, NARROW):
        near_copy(k, lax.rem(n + NARROW - k, NARROW)).wait_recv()
    own[...] = near[...].reshape(NARROW * HUB, TILE).astype(BF)

    def send_hub(o, c):
        hub_copy(o, w).start()
        return c

    lax.fori_loop(1, WIDE, send_hub, 0)
    mine_hub = pltpu.make_async_copy(own, buf.at[hubs_at + w], s_own.at[1])
    mine_hub.start()

    for c in small[3:]:
        c.wait()

    def flat(i):
        return jnp.concatenate([keys[i, pl.ds(r, 1), :] for r in range(TILES // TILE)], axis=1)

    s, d, l = flat(0), flat(1), flat(2)
    lists[0] = tile_list(d, s, l, DST, SRC)
    lists[1] = tile_list(s, d, l, SRC, DST)
    out_lists = [
        pltpu.make_async_copy(lists.at[0], list_f, s_list.at[0]),
        pltpu.make_async_copy(lists.at[1], list_b, s_list.at[1]),
    ]
    for c in out_lists:
        c.start()

    def finish(o, c):
        slot = lax.rem(w + WIDE - o, WIDE)
        row_copy(o, slot).wait()
        hub_copy(o, slot).wait()
        return c

    lax.fori_loop(1, WIDE, finish, 0)
    for k in range(1, NARROW):
        near_copy(k, n).wait_send()
    mine_row.wait()
    mine_hub.wait()
    for c in out_lists:
        c.wait()
    for c in big:
        c.wait()


def in_vmem(x):
    return pltpu.with_memory_space_constraint(x, pltpu.VMEM)


def in_hbm(x):
    return pltpu.with_memory_space_constraint(x, pltpu.HBM)


def fetch(feat, cot, w_self, w_neigh, bias, tiles, src, dst, live, send_rows, hub_rows):
    vmem = pl.BlockSpec(memory_space=pltpu.VMEM)
    hbm = pl.BlockSpec(memory_space=pltpu.HBM)
    dma = pltpu.SemaphoreType.DMA
    return pl.pallas_call(
        fetch_kernel,
        out_shape=(
            pltpu.VMEM((TILES, TILE, TILE), BF),
            pltpu.VMEM(((SRC + 1) * QUADS, SLOT, TILE), BF),
            pltpu.VMEM((DST * TILE, 2 * TILE), BF),
            pltpu.VMEM((2 * TILE, 2 * TILE), BF),
            pltpu.VMEM((1, 2 * TILE), F32),
            pltpu.HBM((4, SLOTS), I32),
            pltpu.HBM((4, SLOTS), I32),
        ),
        in_specs=[hbm] * 11,
        out_specs=(vmem, vmem, vmem, vmem, vmem, hbm, hbm),
        scratch_shapes=[
            pltpu.SMEM((WIDE, SLOT), I32),
            pltpu.SMEM((HUB,), I32),
            pltpu.VMEM((3, TILES // TILE, TILE), I32),
            pltpu.VMEM((DST * TILE, TILE), F32),
            pltpu.VMEM((HUB, TILE), F32),
            pltpu.VMEM((WIDE * SLOT, TILE), F32),
            pltpu.VMEM((WIDE, SLOT, TILE), BF),
            pltpu.VMEM((NARROW, HUB, TILE), F32),
            pltpu.VMEM((NARROW * HUB, TILE), BF),
            pltpu.VMEM((2, 4, SLOTS), I32),
            dma((WIDE,)), dma((WIDE,)), dma((WIDE,)), dma((WIDE,)),
            dma((NARROW,)), dma((NARROW,)), dma((2,)), dma((6,)), dma((4 + CHUNKS,)), dma((2,)),
        ],
        compiler_params=pltpu.CompilerParams(
            collective_id=0, has_side_effects=True, vmem_limit_bytes=VMEM_LIMIT
        ),
    )(
        *map(in_hbm, (feat, cot, w_self, w_neigh, bias, tiles, src, dst, live, send_rows, hub_rows))
    )


def forward_kernel(
    lists_f, wbuf, buf, cotb, w2, bias, hidden, aggregate, grad_pre, list_f, agg, hid, sem, s_hid
):
    load = pltpu.make_async_copy(lists_f, list_f, sem.at[0])
    load.start()

    def clear(i, c):
        agg[i] = jnp.zeros((TILE, TILE), F32)
        return c

    lax.fori_loop(0, DST + 1, clear, 0)
    load.wait()

    def rows_of(s):
        return buf[pl.ds(s * QUADS, QUADS)].reshape(TILE, TILE)

    def step(i, c):
        parts = []
        for u in range(UNROLL):
            k = 2 * (i * UNROLL + u)
            left = jnp.concatenate([wbuf[list_f[0, k]], wbuf[list_f[0, k + 1]]], axis=1)
            right = jnp.concatenate(
                [rows_of(list_f[1, k]), rows_of(list_f[1, k + 1])], axis=0
            )
            parts.append(mm(left, right))
        for u in range(UNROLL):
            agg[list_f[2, 2 * (i * UNROLL + u)]] += parts[u]
        return c

    lax.fori_loop(0, (list_f[3, COUNT] + UNROLL - 1) // UNROLL, step, 0)
    blocks = ROWS // TILE

    def out_hidden(i):
        rows = pl.ds(i * ROWS, ROWS)
        return pltpu.make_async_copy(hid.at[rows, :], hidden.at[rows, :], s_hid.at[i])

    def activate(i, c):
        rows, at = pl.ds(i * ROWS, ROWS), pl.ds(i * blocks, blocks)
        f = buf[pl.ds(i * blocks * QUADS, blocks * QUADS)].reshape(ROWS, TILE)
        a = agg[at].astype(BF)
        aggregate[at] = a
        pre = mm(jnp.concatenate([f, a.reshape(ROWS, TILE)], axis=1), w2[...]) + bias[...]
        square = pre * pre
        t = jnp.tanh(pre * (GELU_A + (GELU_A * GELU_B) * square))
        half = 0.5 + 0.5 * t
        hid[rows, :] = (pre * half).astype(BF)
        out_hidden(i).start()
        slope = half + pre * (0.5 - 0.5 * t * t) * (GELU_A + (3 * GELU_A * GELU_B) * square)
        grad_pre[rows, :] = (cotb[rows, :].astype(F32) * slope).astype(BF)
        return c

    lax.fori_loop(0, DST // blocks, activate, 0)
    for i in range(DST // blocks):
        out_hidden(i).wait()


def forward(list_f, wbuf, buf, cotb, w2, bias):
    vmem = pl.BlockSpec(memory_space=pltpu.VMEM)
    hbm = pl.BlockSpec(memory_space=pltpu.HBM)
    return pl.pallas_call(
        forward_kernel,
        out_shape=(
            jax.ShapeDtypeStruct((DST * TILE, 2 * TILE), BF),
            pltpu.VMEM((DST, TILE, TILE), BF),
            pltpu.VMEM((DST * TILE, 2 * TILE), BF),
        ),
        in_specs=[hbm] + [vmem] * 5,
        out_specs=(hbm, vmem, vmem),
        scratch_shapes=[
            pltpu.SMEM((4, SLOTS), I32),
            pltpu.VMEM((DST + 1, TILE, TILE), F32),
            pltpu.VMEM((DST * TILE, 2 * TILE), BF),
            pltpu.SemaphoreType.DMA((1,)),
            pltpu.SemaphoreType.DMA((DST * TILE // ROWS,)),
        ],
        compiler_params=pltpu.CompilerParams(vmem_limit_bytes=VMEM_LIMIT),
    )(in_hbm(list_f), *map(in_vmem, (wbuf, buf, cotb, w2, bias)))


def backward_kernel(
    lists_b, hub_rows, send_rows, wbuf, buf, w2, aggregate, grad_pre, acc, whole, total_bias,
    list_b, hub_at, send_at, slots, gt, wg, gb, sums, bound, hubs,
    back, sum_in, hub_in, sum_out, sum_near, hub_out, hub_near, part,
    s_back, r_back, s_sum, r_sum, s_hub, r_hub, s_part, r_part,
    s_sum_near, r_sum_near, s_hub_near, r_hub_near, s_in,
):
    w = lax.axis_index("wide")
    n = lax.axis_index("narrow")
    loads = [
        pltpu.make_async_copy(lists_b, list_b, s_in.at[0]),
        pltpu.make_async_copy(hub_rows, hub_at, s_in.at[1]),
        pltpu.make_async_copy(send_rows, send_at, s_in.at[2]),
    ]
    for c in loads:
        c.start()
    barrier = greet_all(w, n)
    gb[...] = jnp.zeros_like(gb)
    wg[...] = jnp.zeros_like(wg)
    gt[DST] = jnp.zeros((TILE, TILE), BF)
    slots[PAIRS] = jnp.zeros((TILE, TILE), F32)
    blocks = ROWS // TILE

    def dense(i, c):
        rows = pl.ds(i * ROWS, ROWS)
        f = buf[pl.ds(i * blocks * QUADS, blocks * QUADS)].reshape(ROWS, TILE)
        x = jnp.concatenate([f, aggregate[pl.ds(i * blocks, blocks)].reshape(ROWS, TILE)], axis=1)
        gp = grad_pre[rows, :]
        wg[...] += tn(x, gp)
        gb[...] += jnp.sum(gp.astype(F32).reshape(ROWS // 8, 8, 2 * TILE), axis=0)
        acc[rows, :] = nt(gp, w2[pl.ds(0, TILE), :])
        g = nt(w2[pl.ds(TILE, TILE), :], gp).astype(BF)
        for j in range(blocks):
            gt[i * blocks + j] = g[:, j * TILE : (j + 1) * TILE]
        return c

    lax.fori_loop(0, DST // blocks, dense, 0)
    bias_sum = jnp.sum(gb[...], axis=0, keepdims=True)
    row = iota((16, TILE), 0)
    bias_rows = jnp.where(
        row == 0, bias_sum[:, :TILE], jnp.where(row == 1, bias_sum[:, TILE:], 0.0)
    ).astype(BF)
    for p in range(WIDE):
        rows = wg[pl.ds(8 * p, 8), :]
        sums[p, pl.ds(0, 16), :] = jnp.concatenate(
            [rows[:, :TILE], rows[:, TILE:]], axis=0
        ).astype(BF)
        sums[p, pl.ds(16, 16), :] = bias_rows
    pl.semaphore_wait(barrier, WIDE - 1 + NARROW - 1)

    def wide_copy(o, src, dst, send, recv):
        return pltpu.make_async_remote_copy(
            src_ref=src,
            dst_ref=dst,
            send_sem=send.at[o],
            recv_sem=recv.at[o],
            device_id=(lax.rem(w + o, WIDE), n),
            device_id_type=MESH,
        )

    def near_copy(k, src, dst, send, recv):
        return pltpu.make_async_remote_copy(
            src_ref=src,
            dst_ref=dst,
            send_sem=send.at[k],
            recv_sem=recv.at[k],
            device_id=(w, lax.rem(n + k, NARROW)),
            device_id_type=MESH,
        )

    def sum_copy(o, slot):
        return wide_copy(o, sums.at[lax.rem(w + o, WIDE)], sum_in.at[slot], s_sum, r_sum)

    def hub_copy(o, slot):
        return wide_copy(o, hubs.at[lax.rem(w + o, WIDE)], hub_in.at[slot], s_hub, r_hub)

    def back_copy(o, slot):
        return wide_copy(o, bound.at[lax.rem(w + o, WIDE)], back.at[slot], s_back, r_back)

    def part_copy(o, slot):
        return wide_copy(o, part, whole.at[slot], s_part, r_part)

    def sum_near_copy(k, slot):
        return near_copy(k, sum_out, sum_near.at[slot], s_sum_near, r_sum_near)

    def hub_near_copy(k, slot):
        peer = lax.rem(n + k, NARROW)
        return near_copy(k, hub_out.at[peer], hub_near.at[slot], s_hub_near, r_hub_near)

    def send(copy):
        def one(o, c):
            copy(o, w).start()
            return c

        lax.fori_loop(1, WIDE, one, 0)

    def arrive(copy):
        def one(o, c):
            copy(o, lax.rem(w + WIDE - o, WIDE)).wait_recv()
            return c

        lax.fori_loop(1, WIDE, one, 0)

    def near_arrive(copy):
        for k in range(1, NARROW):
            copy(k, lax.rem(n + NARROW - k, NARROW)).wait_recv()

    def add_up(ref, rows):
        def one(q, total):
            return total + ref[q].astype(F32)

        return lax.fori_loop(0, WIDE, one, jnp.zeros((rows, TILE), F32))

    def walk(i, total):
        parts = []
        for u in range(UNROLL):
            k = 2 * (i * UNROLL + u)
            left = jnp.concatenate([gt[list_b[1, k]], gt[list_b[1, k + 1]]], axis=1)
            right = jnp.concatenate([wbuf[list_b[0, k]], wbuf[list_b[0, k + 1]]], axis=0)
            parts.append(mm(left, right))
        for u in range(UNROLL):
            k = i * UNROLL + u
            same = list_b[2, 2 * k] == list_b[2, jnp.maximum(2 * k - 2, 0)]
            total = total * same.astype(F32) + parts[u]
            slots[k] = total
        return total

    send(sum_copy)
    sum_in[w] = sums[w]
    for c in loads:
        c.wait()
    steps = PAIRS // UNROLL
    total = lax.fori_loop(0, steps // 2, walk, jnp.zeros((TILE, TILE), F32))
    arrive(sum_copy)
    sum_out[...] = add_up(sum_in, SLOT)[:24]
    sum_near[n] = sum_out[...]
    for k in range(1, NARROW):
        sum_near_copy(k, n).start()
    lax.fori_loop(steps // 2, steps, walk, total)
    near_arrive(sum_near_copy)
    near = sum_near[0] + sum_near[1] + sum_near[2] + sum_near[3]
    part[...] = near[0:16].astype(BF)
    whole[w] = near[0:16].astype(BF)
    total_bias[...] = near[16:24]

    remote = WIDE // QUADS
    for i in range(remote):
        at = pl.ds(i * QUADS, QUADS)
        total = slots[list_b[3, DST + remote + i]]
        hubs[at] = total.T.astype(BF).reshape(QUADS, SLOT, TILE)
    send(hub_copy)
    for i in range(remote):
        at = pl.ds(i * QUADS, QUADS)
        total = slots[list_b[3, DST + i]]
        bound[at] = total.T.astype(BF).reshape(QUADS, SLOT, TILE)
    send(back_copy)
    send(part_copy)
    hub_in[w] = hubs[w]
    back[w] = bound[w]

    def add_own(i, c):
        at = pl.ds(i * TILE, TILE)
        acc[at, :] += slots[list_b[3, i]].T
        return c

    lax.fori_loop(0, DST, add_own, 0, unroll=4)
    lane = iota((1, TILE), 1)
    hub_lane = jnp.full((1, TILE), -1, I32)
    for j in range(HUB):
        hub_lane = jnp.where((lane == j) | (lane == j + HUB), hub_at[j], hub_lane)
    row_lane = jnp.concatenate([send_at[pl.ds(p, 1), :] for p in range(WIDE)], axis=1)

    arrive(hub_copy)
    hub_sum = add_up(hub_in, SLOT)
    for k in range(NARROW):
        hub_out[k] = hub_sum[HUB * k : HUB * (k + 1)]
    hub_near[n] = hub_out[n]
    for k in range(1, NARROW):
        hub_near_copy(k, n).start()

    def scatter(lanes, values):
        step = 512

        def one(i, c):
            at = pl.ds(i * step, step)
            hit = iota((step, lanes.shape[1]), 0) + i * step == lanes
            acc[at, :] += mm(jnp.where(hit, 1.0, 0.0).astype(BF), values)
            return c

        lax.fori_loop(0, DST * TILE // step, one, 0)

    arrive(back_copy)
    scatter(row_lane, back[...].reshape(WIDE * SLOT, TILE))
    near_arrive(hub_near_copy)
    mine = hub_near[0] + hub_near[1] + hub_near[2] + hub_near[3]
    high = mine.astype(BF)
    low = (mine - high.astype(F32)).astype(BF)
    values = jnp.concatenate([high, low, jnp.zeros((TILE - 2 * HUB, TILE), BF)], axis=0)
    scatter(hub_lane, values)
    arrive(part_copy)

    def sent(o, c):
        sum_copy(o, w).wait_send()
        hub_copy(o, w).wait_send()
        back_copy(o, w).wait_send()
        part_copy(o, w).wait_send()
        return c

    lax.fori_loop(1, WIDE, sent, 0)
    for k in range(1, NARROW):
        sum_near_copy(k, n).wait_send()
        hub_near_copy(k, n).wait_send()


def backward(list_b, hub_rows, send_rows, wbuf, buf, w2, aggregate, grad_pre):
    vmem = pl.BlockSpec(memory_space=pltpu.VMEM)
    hbm = pl.BlockSpec(memory_space=pltpu.HBM)
    dma = pltpu.SemaphoreType.DMA
    return pl.pallas_call(
        backward_kernel,
        out_shape=(
            pltpu.VMEM((DST * TILE, TILE), F32),
            pltpu.VMEM((WIDE, 16, TILE), BF),
            pltpu.VMEM((8, TILE), F32),
        ),
        in_specs=[hbm] * 3 + [vmem] * 5,
        out_specs=(vmem,) * 3,
        scratch_shapes=[
            pltpu.SMEM((4, SLOTS), I32),
            pltpu.SMEM((HUB,), I32),
            pltpu.VMEM((WIDE, SLOT), I32),
            pltpu.VMEM((PAIRS + 1, TILE, TILE), F32),
            pltpu.VMEM((DST + 1, TILE, TILE), BF),
            pltpu.VMEM((2 * TILE, 2 * TILE), F32),
            pltpu.VMEM((8, 2 * TILE), F32),
            pltpu.VMEM((WIDE, SLOT, TILE), BF),
            pltpu.VMEM((WIDE, SLOT, TILE), BF),
            pltpu.VMEM((WIDE, SLOT, TILE), BF),
            pltpu.VMEM((WIDE, SLOT, TILE), BF),
            pltpu.VMEM((WIDE, SLOT, TILE), BF),
            pltpu.VMEM((WIDE, SLOT, TILE), BF),
            pltpu.VMEM((24, TILE), F32),
            pltpu.VMEM((NARROW, 24, TILE), F32),
            pltpu.VMEM((NARROW, HUB, TILE), F32),
            pltpu.VMEM((NARROW, HUB, TILE), F32),
            pltpu.VMEM((16, TILE), BF),
            dma((WIDE,)), dma((WIDE,)), dma((WIDE,)), dma((WIDE,)),
            dma((WIDE,)), dma((WIDE,)), dma((WIDE,)), dma((WIDE,)),
            dma((NARROW,)), dma((NARROW,)), dma((NARROW,)), dma((NARROW,)), dma((3,)),
        ],
        compiler_params=pltpu.CompilerParams(
            collective_id=1, has_side_effects=True, vmem_limit_bytes=VMEM_LIMIT
        ),
    )(
        in_hbm(list_b), in_hbm(hub_rows), in_hbm(send_rows),
        *map(in_vmem, (wbuf, buf, w2, aggregate, grad_pre)),
    )


def finish_kernel(acc, whole, total_bias, gfeat, g_self, g_neigh, g_bias, weights, bias, sem):
    store = pltpu.make_async_copy(acc, gfeat, sem.at[0])
    store.start()
    for p in range(WIDE):
        got = whole[p].astype(F32)
        weights[pl.ds(8 * p, 8), :] = jnp.concatenate([got[:8], got[8:]], axis=1)
    bias[...] = jnp.concatenate([total_bias[pl.ds(0, 1), :], total_bias[pl.ds(1, 1), :]], axis=1)
    outs = [
        pltpu.make_async_copy(weights.at[pl.ds(0, TILE)], g_self, sem.at[1]),
        pltpu.make_async_copy(weights.at[pl.ds(TILE, TILE)], g_neigh, sem.at[2]),
        pltpu.make_async_copy(bias, g_bias, sem.at[3]),
    ]
    for c in outs:
        c.start()
    for c in [store] + outs:
        c.wait()


def finish(acc, whole, total_bias):
    vmem = pl.BlockSpec(memory_space=pltpu.VMEM)
    hbm = pl.BlockSpec(memory_space=pltpu.HBM)
    return pl.pallas_call(
        finish_kernel,
        out_shape=(
            jax.ShapeDtypeStruct((DST * TILE, TILE), F32),
            jax.ShapeDtypeStruct((TILE, 2 * TILE), F32),
            jax.ShapeDtypeStruct((TILE, 2 * TILE), F32),
            jax.ShapeDtypeStruct((1, 2 * TILE), F32),
        ),
        in_specs=[vmem] * 3,
        out_specs=(hbm,) * 4,
        scratch_shapes=[
            pltpu.VMEM((2 * TILE, 2 * TILE), F32),
            pltpu.VMEM((1, 2 * TILE), F32),
            pltpu.SemaphoreType.DMA((4,)),
        ],
    )(in_vmem(acc), in_vmem(whole), in_vmem(total_bias))


def on_device(
    features, cotangent, w_self, w_neigh, bias, tile_weights, tile_src, tile_dst, tile_live,
    send_rows, hub_rows,
):
    lanes = (TILES // TILE, TILE)
    wbuf, buf, cotb, w2, b2, list_f, list_b = fetch(
        features.reshape(DST * QUADS, SLOT, TILE), cotangent, w_self, w_neigh,
        bias.reshape(1, 2 * TILE), tile_weights,
        tile_src.reshape(lanes), tile_dst.reshape(lanes), tile_live.reshape(lanes),
        send_rows, hub_rows,
    )
    hidden, aggregate, grad_pre = forward(list_f, wbuf, buf, cotb, w2, b2)
    acc, whole, total_bias = backward(
        list_b, hub_rows, send_rows, wbuf, buf, w2, aggregate, grad_pre
    )
    grad_features, grad_self, grad_neigh, grad_bias = finish(acc, whole, total_bias)
    return (hidden, grad_features, grad_self, grad_neigh, grad_bias.reshape(2 * TILE))


def solution(mesh):
    both = ("wide", "narrow")
    placed = (
        P(both, None), P(both, None), P(), P(), P(), P(both, None, None),
        P(both), P(both), P(both), P(both, None), P(both),
    )
    return jax.shard_map(
        on_device,
        mesh=mesh,
        in_specs=placed,
        out_specs=(P(both, None), P(both, None), P(), P(), P()),
        check_vma=False,
    )
```

```python
import functools

import jax
import jax.numpy as jnp
from jax import lax
from jax.experimental import pallas as pl
from jax.experimental.pallas import tpu as pltpu
from jax.sharding import PartitionSpec as P

MESH = pl.DeviceIdType.MESH
BF, F32, I32 = jnp.bfloat16, jnp.float32, jnp.int32
TILE = 128
DST = 32
SRC = 48
TILES = 512
SLOTS = 640
UNROLL = 24
WALK = 34
PAIRS = 272
COUNT = 64
ROWS = 1024
CHUNKS = 8
VMEM_LIMIT = 32 * 2**20
SLOT = 32
QUADS = TILE // SLOT
HUB = 8
WIDE = 32
NARROW = 4
GELU_A = 0.7978845608028654
GELU_B = 0.044715


def mm(a, b):
    return jnp.dot(a, b, preferred_element_type=F32)


def nt(a, b):
    return lax.dot_general(a, b, (((1,), (1,)), ((), ())), preferred_element_type=F32)


def tn(a, b):
    return lax.dot_general(a, b, (((0,), (0,)), ((), ())), preferred_element_type=F32)


def iota(shape, dim):
    return lax.broadcasted_iota(I32, shape, dim)


def tile_list(key, other, live, keys, zero):
    groups = 64
    hot = jnp.where((iota((groups, TILES), 0) == key) & (live > 0), 1.0, 0.0)
    before = jnp.where(iota((TILES, TILES), 0) < iota((TILES, TILES), 1), 1.0, 0.0).astype(BF)
    rank = mm(hot.astype(BF), before)
    count = jnp.sum(hot, axis=1, keepdims=True).astype(I32)
    even = ((count + 1) // 2 * 2).astype(F32)
    lower = jnp.where(iota((groups, groups), 1) < iota((groups, groups), 0), 1.0, 0.0).astype(BF)
    start = mm(lower, jnp.broadcast_to(even, (groups, TILE)).astype(BF))[:, :1]
    total = jnp.sum(even, axis=0, keepdims=True)
    place = jnp.sum(hot * (rank + start), axis=0, keepdims=True).astype(I32)
    place = jnp.where(live > 0, place, -1)
    at = jnp.where(iota((SLOTS, TILES), 0) == place, 1.0, 0.0).astype(BF)
    t = iota((1, TILES), 1)
    rows = [t // 16, t % 16, other - zero, key - keys]
    row = iota((8, TILES), 0)
    values = jnp.zeros((8, TILES), I32)
    for r, v in enumerate(rows):
        values = jnp.where(row == r, v, values)
    got = nt(values.astype(F32).astype(BF), at).astype(I32)
    last = jnp.where(even > 0, (start + even) * 0.5 - 1.0, float(PAIRS))
    across = iota((groups, TILE), 0) == iota((groups, TILE), 1)
    last = jnp.sum(jnp.where(across, last, 0.0), axis=0, keepdims=True)
    info = jnp.where(iota((1, TILE), 1) < groups, last, total * 0.5).astype(I32)
    return jnp.concatenate(
        [
            got[0:1] * 16 + got[1:2],
            got[2:3] + zero,
            got[3:4] + keys,
            jnp.concatenate([info, jnp.zeros((1, SLOTS - TILE), I32)], axis=1),
        ],
        axis=0,
    )


def greet_all(w, n):
    barrier = pltpu.get_barrier_semaphore()

    def greet(o, c):
        pl.semaphore_signal(
            barrier, inc=1, device_id=(lax.rem(w + o, WIDE), n), device_id_type=MESH
        )
        return c

    lax.fori_loop(1, WIDE, greet, 0)
    for k in range(1, NARROW):
        pl.semaphore_signal(
            barrier, inc=1, device_id=(w, lax.rem(n + k, NARROW)), device_id_type=MESH
        )
    return barrier


def fetch_kernel(
    feat, w_self, w_neigh, bias, tiles, src, dst, live, send_rows, hub_rows,
    wbuf, buf, w2, b2, list_f, list_r, list_o,
    send_at, hub_at, keys, wide32, hubs, picked, msg, near, own, lists,
    s_row, r_row, s_hub, r_hub, s_near, r_near, s_own, s_in, s_big, s_list,
):
    w = lax.axis_index("wide")
    n = lax.axis_index("narrow")
    small = [
        pltpu.make_async_copy(send_rows, send_at, s_in.at[0]),
        pltpu.make_async_copy(hub_rows, hub_at, s_in.at[1]),
        pltpu.make_async_copy(feat, buf.at[pl.ds(0, DST * QUADS)], s_in.at[2]),
        pltpu.make_async_copy(src, keys.at[0], s_in.at[3]),
        pltpu.make_async_copy(dst, keys.at[1], s_in.at[4]),
        pltpu.make_async_copy(live, keys.at[2], s_in.at[5]),
    ]
    for c in small:
        c.start()
    barrier = greet_all(w, n)
    big = [
        pltpu.make_async_copy(w_self, w2.at[pl.ds(0, TILE)], s_big.at[0]),
        pltpu.make_async_copy(w_neigh, w2.at[pl.ds(TILE, TILE)], s_big.at[1]),
        pltpu.make_async_copy(bias, b2, s_big.at[2]),
    ]
    per = TILES // CHUNKS
    big += [
        pltpu.make_async_copy(
            tiles.at[pl.ds(i * per, per)], wbuf.at[pl.ds(i * per, per)], s_big.at[3 + i]
        )
        for i in range(CHUNKS)
    ]
    for c in big:
        c.start()
    buf[pl.ds(SRC * QUADS, QUADS)] = jnp.zeros((QUADS, SLOT, TILE), BF)
    for c in small[:3]:
        c.wait()
    wide32[...] = buf[pl.ds(0, DST * QUADS)].astype(F32).reshape(DST * TILE, TILE)
    for j in range(HUB):
        hubs[pl.ds(j, 1), :] = wide32[pl.ds(hub_at[j], 1), :]

    def pick(p, c):
        for j in range(SLOT):
            picked[pl.ds(p * SLOT + j, 1), :] = wide32[pl.ds(send_at[p, j], 1), :]
        return c

    lax.fori_loop(0, WIDE, pick, 0)
    msg[...] = picked[...].astype(BF).reshape(WIDE, SLOT, TILE)
    near[n] = hubs[...]

    pl.semaphore_wait(barrier, WIDE - 1 + NARROW - 1)
    rows_at, hubs_at = DST * QUADS, DST * QUADS + WIDE

    def near_copy(k, slot):
        return pltpu.make_async_remote_copy(
            src_ref=hubs,
            dst_ref=near.at[slot],
            send_sem=s_near.at[k],
            recv_sem=r_near.at[k],
            device_id=(w, lax.rem(n + k, NARROW)),
            device_id_type=MESH,
        )

    def row_copy(o, slot):
        p = lax.rem(w + o, WIDE)
        return pltpu.make_async_remote_copy(
            src_ref=msg.at[p],
            dst_ref=buf.at[rows_at + slot],
            send_sem=s_row.at[o],
            recv_sem=r_row.at[o],
            device_id=(p, n),
            device_id_type=MESH,
        )

    def hub_copy(o, slot):
        return pltpu.make_async_remote_copy(
            src_ref=own,
            dst_ref=buf.at[hubs_at + slot],
            send_sem=s_hub.at[o],
            recv_sem=r_hub.at[o],
            device_id=(lax.rem(w + o, WIDE), n),
            device_id_type=MESH,
        )

    for k in range(1, NARROW):
        near_copy(k, n).start()

    def send_row(o, c):
        row_copy(o, w).start()
        return c

    lax.fori_loop(1, WIDE, send_row, 0)
    mine_row = pltpu.make_async_copy(msg.at[w], buf.at[rows_at + w], s_own.at[0])
    mine_row.start()
    for k in range(1, NARROW):
        near_copy(k, lax.rem(n + NARROW - k, NARROW)).wait_recv()
    own[...] = near[...].reshape(NARROW * HUB, TILE).astype(BF)

    def send_hub(o, c):
        hub_copy(o, w).start()
        return c

    lax.fori_loop(1, WIDE, send_hub, 0)
    mine_hub = pltpu.make_async_copy(own, buf.at[hubs_at + w], s_own.at[1])
    mine_hub.start()

    for c in small[3:]:
        c.wait()

    def flat(i):
        return jnp.concatenate([keys[i, pl.ds(r, 1), :] for r in range(TILES // TILE)], axis=1)

    s, d, l = flat(0), flat(1), flat(2)
    lists[0] = tile_list(d, s, l, DST, SRC)
    lists[1] = tile_list(s - DST, d, jnp.where(s >= DST, l, 0), SRC - DST, DST)
    lists[2] = tile_list(s, d, jnp.where(s < DST, l, 0), DST, DST)
    out_lists = [
        pltpu.make_async_copy(lists.at[i], out, s_list.at[i])
        for i, out in enumerate((list_f, list_r, list_o))
    ]
    for c in out_lists:
        c.start()

    def finish(o, c):
        slot = lax.rem(w + WIDE - o, WIDE)
        row_copy(o, slot).wait()
        hub_copy(o, slot).wait()
        return c

    lax.fori_loop(1, WIDE, finish, 0)
    for k in range(1, NARROW):
        near_copy(k, n).wait_send()
    mine_row.wait()
    mine_hub.wait()
    for c in out_lists:
        c.wait()
    for c in big:
        c.wait()


def in_vmem(x):
    return pltpu.with_memory_space_constraint(x, pltpu.VMEM)


def in_hbm(x):
    return pltpu.with_memory_space_constraint(x, pltpu.HBM)


def fetch(*args):
    vmem = pl.BlockSpec(memory_space=pltpu.VMEM)
    hbm = pl.BlockSpec(memory_space=pltpu.HBM)
    dma = pltpu.SemaphoreType.DMA
    return pl.pallas_call(
        fetch_kernel,
        out_shape=(
            pltpu.VMEM((TILES, TILE, TILE), BF),
            pltpu.VMEM(((SRC + 1) * QUADS, SLOT, TILE), BF),
            pltpu.VMEM((2 * TILE, 2 * TILE), BF),
            pltpu.VMEM((1, 2 * TILE), F32),
            pltpu.HBM((4, SLOTS), I32),
            pltpu.HBM((4, SLOTS), I32),
            pltpu.HBM((4, SLOTS), I32),
        ),
        in_specs=[hbm] * 10,
        out_specs=(vmem,) * 4 + (hbm,) * 3,
        scratch_shapes=[
            pltpu.SMEM((WIDE, SLOT), I32),
            pltpu.SMEM((HUB,), I32),
            pltpu.VMEM((3, TILES // TILE, TILE), I32),
            pltpu.VMEM((DST * TILE, TILE), F32),
            pltpu.VMEM((HUB, TILE), F32),
            pltpu.VMEM((WIDE * SLOT, TILE), F32),
            pltpu.VMEM((WIDE, SLOT, TILE), BF),
            pltpu.VMEM((NARROW, HUB, TILE), F32),
            pltpu.VMEM((NARROW * HUB, TILE), BF),
            pltpu.VMEM((3, 4, SLOTS), I32),
            dma((WIDE,)), dma((WIDE,)), dma((WIDE,)), dma((WIDE,)),
            dma((NARROW,)), dma((NARROW,)), dma((2,)), dma((6,)), dma((3 + CHUNKS,)), dma((3,)),
        ],
        compiler_params=pltpu.CompilerParams(
            collective_id=0, has_side_effects=True, vmem_limit_bytes=VMEM_LIMIT
        ),
    )(*map(in_hbm, args))


def forward_kernel(
    lists_f, lists_r, cot, wbuf, buf, w2, bias, hidden, grad_pre, gt, sums, bound, hub_out,
    list_f, list_r, cotb, agg, hid, gbt, wg, gb, sem, s_hid,
):
    loads = [
        pltpu.make_async_copy(lists_f, list_f, sem.at[0]),
        pltpu.make_async_copy(lists_r, list_r, sem.at[1]),
        pltpu.make_async_copy(cot, cotb, sem.at[2]),
    ]
    for c in loads:
        c.start()

    def clear(i, c):
        agg[i] = jnp.zeros((TILE, TILE), F32)
        return c

    lax.fori_loop(0, DST + 1, clear, 0)
    loads[0].wait()

    def rows_of(s):
        return buf[pl.ds(s * QUADS, QUADS)].reshape(TILE, TILE)

    def step(i, c):
        parts = []
        for u in range(UNROLL):
            k = 2 * (i * UNROLL + u)
            left = jnp.concatenate([wbuf[list_f[0, k]], wbuf[list_f[0, k + 1]]], axis=1)
            right = jnp.concatenate(
                [rows_of(list_f[1, k]), rows_of(list_f[1, k + 1])], axis=0
            )
            parts.append(mm(left, right))
        for u in range(UNROLL):
            agg[list_f[2, 2 * (i * UNROLL + u)]] += parts[u]
        return c

    lax.fori_loop(0, (list_f[3, COUNT] + UNROLL - 1) // UNROLL, step, 0)
    def clear_back(i, c):
        gbt[i] = jnp.zeros((TILE, TILE), F32)
        return c

    lax.fori_loop(0, SRC - DST + 1, clear_back, 0)
    gb[...] = jnp.zeros_like(gb)
    wg[...] = jnp.zeros_like(wg)
    gt[DST] = jnp.zeros((TILE, TILE), BF)
    for c in loads[1:]:
        c.wait()
    blocks = ROWS // TILE

    def out_hidden(i):
        rows = pl.ds(i * ROWS, ROWS)
        return pltpu.make_async_copy(hid.at[rows, :], hidden.at[rows, :], s_hid.at[i])

    def activate(i, c):
        rows, at = pl.ds(i * ROWS, ROWS), pl.ds(i * blocks, blocks)
        f = buf[pl.ds(i * blocks * QUADS, blocks * QUADS)].reshape(ROWS, TILE)
        a = agg[at].reshape(ROWS, TILE).astype(BF)
        x = jnp.concatenate([f, a], axis=1)
        pre = mm(x, w2[...]) + bias[...]
        square = pre * pre
        t = jnp.tanh(pre * (GELU_A + (GELU_A * GELU_B) * square))
        half = 0.5 + 0.5 * t
        hid[rows, :] = (pre * half).astype(BF)
        out_hidden(i).start()
        slope = half + pre * (0.5 - 0.5 * t * t) * (GELU_A + (3 * GELU_A * GELU_B) * square)
        gp = (cotb[rows, :].astype(F32) * slope).astype(BF)
        grad_pre[rows, :] = gp
        wg[...] += tn(x, gp)
        gb[...] += jnp.sum(gp.astype(F32).reshape(ROWS // 8, 8, 2 * TILE), axis=0)
        g = nt(w2[pl.ds(TILE, TILE), :], gp).astype(BF)
        for j in range(blocks):
            gt[i * blocks + j] = g[:, j * TILE : (j + 1) * TILE]
        return c

    lax.fori_loop(0, DST // blocks, activate, 0)

    def step_back(i, c):
        parts = []
        for u in range(UNROLL):
            k = 2 * (i * UNROLL + u)
            left = jnp.concatenate([gt[list_r[1, k]], gt[list_r[1, k + 1]]], axis=1)
            right = jnp.concatenate([wbuf[list_r[0, k]], wbuf[list_r[0, k + 1]]], axis=0)
            parts.append(mm(left, right))
        for u in range(UNROLL):
            gbt[list_r[2, 2 * (i * UNROLL + u)]] += parts[u]
        return c

    lax.fori_loop(0, (list_r[3, COUNT] + UNROLL - 1) // UNROLL, step_back, 0)
    bias_sum = jnp.sum(gb[...], axis=0, keepdims=True)
    row = iota((16, TILE), 0)
    bias_rows = jnp.where(
        row == 0, bias_sum[:, :TILE], jnp.where(row == 1, bias_sum[:, TILE:], 0.0)
    ).astype(BF)
    for k in range(NARROW):
        hub_out[k, pl.ds(WIDE * HUB, 16), :] = bias_rows
    for p in range(WIDE):
        rows = wg[pl.ds(8 * p, 8), :]
        sums[p] = jnp.concatenate(
            [rows[:, :TILE], rows[:, TILE:]], axis=0
        ).astype(BF)
    remote = WIDE // QUADS
    for i in range(remote):
        at = pl.ds(i * QUADS, QUADS)
        bound[at] = gbt[i].T.astype(BF).reshape(QUADS, SLOT, TILE)
        total = gbt[remote + i].T
        for k in range(NARROW):
            rows = [total[q * SLOT + k * HUB :][:HUB] for q in range(QUADS)]
            hub_out[k, pl.ds(i * SLOT, SLOT), :] = jnp.concatenate(rows, axis=0).astype(BF)
    for i in range(DST // blocks):
        out_hidden(i).wait()


def forward(list_f, list_r, cot, wbuf, buf, w2, bias):
    vmem = pl.BlockSpec(memory_space=pltpu.VMEM)
    hbm = pl.BlockSpec(memory_space=pltpu.HBM)
    return pl.pallas_call(
        forward_kernel,
        out_shape=(
            jax.ShapeDtypeStruct((DST * TILE, 2 * TILE), BF),
            pltpu.VMEM((DST * TILE, 2 * TILE), BF),
            pltpu.VMEM((DST + 1, TILE, TILE), BF),
            pltpu.VMEM((WIDE, 16, TILE), BF),
            pltpu.VMEM((WIDE, SLOT, TILE), BF),
            pltpu.VMEM((NARROW, WIDE * HUB + 16, TILE), BF),
        ),
        in_specs=[hbm] * 3 + [vmem] * 4,
        out_specs=(hbm,) + (vmem,) * 5,
        scratch_shapes=[
            pltpu.SMEM((4, SLOTS), I32),
            pltpu.SMEM((4, SLOTS), I32),
            pltpu.VMEM((DST * TILE, 2 * TILE), BF),
            pltpu.VMEM((DST + 1, TILE, TILE), F32),
            pltpu.VMEM((DST * TILE, 2 * TILE), BF),
            pltpu.VMEM((SRC - DST + 1, TILE, TILE), F32),
            pltpu.VMEM((2 * TILE, 2 * TILE), F32),
            pltpu.VMEM((8, 2 * TILE), F32),
            pltpu.SemaphoreType.DMA((3,)),
            pltpu.SemaphoreType.DMA((DST * TILE // ROWS,)),
        ],
        compiler_params=pltpu.CompilerParams(vmem_limit_bytes=VMEM_LIMIT),
    )(*map(in_hbm, (list_f, list_r, cot)), *map(in_vmem, (wbuf, buf, w2, bias)))


def backward_kernel(
    lists_o, hub_rows, send_rows, wbuf, w2, grad_pre, gt, sums, bound, hub_out,
    acc, whole, total_bias,
    list_o, hub_at, send_at, slots, back, sum_in, hub_in, sum_out, sum_near, hub_near, hub_part,
    part, s_back, r_back, s_sum, r_sum, s_hub, r_hub, s_part, r_part,
    s_sum_near, r_sum_near, s_hub_near, r_hub_near, s_in,
):
    w = lax.axis_index("wide")
    n = lax.axis_index("narrow")
    loads = [
        pltpu.make_async_copy(lists_o, list_o, s_in.at[0]),
        pltpu.make_async_copy(hub_rows, hub_at, s_in.at[1]),
        pltpu.make_async_copy(send_rows, send_at, s_in.at[2]),
    ]
    for c in loads:
        c.start()
    barrier = greet_all(w, n)
    slots[PAIRS] = jnp.zeros((TILE, TILE), F32)

    pl.semaphore_wait(barrier, WIDE - 1 + NARROW - 1)

    def wide_copy(o, src, dst, send, recv):
        return pltpu.make_async_remote_copy(
            src_ref=src,
            dst_ref=dst,
            send_sem=send.at[o],
            recv_sem=recv.at[o],
            device_id=(lax.rem(w + o, WIDE), n),
            device_id_type=MESH,
        )

    def near_copy(k, src, dst, send, recv):
        return pltpu.make_async_remote_copy(
            src_ref=src,
            dst_ref=dst,
            send_sem=send.at[k],
            recv_sem=recv.at[k],
            device_id=(w, lax.rem(n + k, NARROW)),
            device_id_type=MESH,
        )

    def sum_copy(o, slot):
        return wide_copy(o, sums.at[lax.rem(w + o, WIDE)], sum_in.at[slot], s_sum, r_sum)

    def hub_copy(o, slot):
        return wide_copy(o, hub_part.at[lax.rem(w + o, WIDE)], hub_in.at[slot], s_hub, r_hub)

    def back_copy(o, slot):
        return wide_copy(o, bound.at[lax.rem(w + o, WIDE)], back.at[slot], s_back, r_back)

    def part_copy(o, slot):
        return wide_copy(o, part, whole.at[slot], s_part, r_part)

    def sum_near_copy(k, slot):
        return near_copy(k, sum_out, sum_near.at[slot], s_sum_near, r_sum_near)

    def hub_near_copy(k, slot):
        peer = lax.rem(n + k, NARROW)
        return near_copy(k, hub_out.at[peer], hub_near.at[slot], s_hub_near, r_hub_near)

    def send(copy):
        def one(o, c):
            copy(o, w).start()
            return c

        lax.fori_loop(1, WIDE, one, 0)

    def arrive(copy):
        def one(o, c):
            copy(o, lax.rem(w + WIDE - o, WIDE)).wait_recv()
            return c

        lax.fori_loop(1, WIDE, one, 0)

    def near_arrive(copy):
        for k in range(1, NARROW):
            copy(k, lax.rem(n + NARROW - k, NARROW)).wait_recv()

    def add_up(ref, rows):
        def one(q, total):
            return total + ref[q].astype(F32)

        return lax.fori_loop(0, WIDE, one, jnp.zeros((rows, TILE), F32), unroll=4)

    def walk(i, total):
        parts = []
        for u in range(WALK):
            k = 2 * (i * WALK + u)
            left = jnp.concatenate([gt[list_o[1, k]], gt[list_o[1, k + 1]]], axis=1)
            right = jnp.concatenate([wbuf[list_o[0, k]], wbuf[list_o[0, k + 1]]], axis=0)
            parts.append(mm(left, right))
        for u in range(WALK):
            k = i * WALK + u
            same = list_o[2, 2 * k] == list_o[2, jnp.maximum(2 * k - 2, 0)]
            total = total * same.astype(F32) + parts[u]
            slots[k] = total
        return total

    send(sum_copy)
    for k in range(1, NARROW):
        hub_near_copy(k, n).start()
    send(back_copy)
    sum_in[w] = sums[w]
    back[w] = bound[w]
    hub_near[n] = hub_out[n]
    for c in loads:
        c.wait()
    def own_part(i, c):
        rows = pl.ds(i * ROWS, ROWS)
        acc[rows, :] = nt(grad_pre[rows, :], w2[pl.ds(0, TILE), :])
        return c

    lax.fori_loop(0, DST * TILE // ROWS, own_part, 0)
    lax.fori_loop(0, PAIRS // WALK, walk, jnp.zeros((TILE, TILE), F32))

    arrive(sum_copy)
    sum_out[...] = add_up(sum_in, 16)
    sum_near[n] = sum_out[...]
    for k in range(1, NARROW):
        sum_near_copy(k, n).start()
    near_arrive(hub_near_copy)
    hub_sum = sum(hub_near[k].astype(F32) for k in range(NARROW))
    hub_part[:, pl.ds(0, HUB), :] = hub_sum[: WIDE * HUB].reshape(WIDE, HUB, TILE)
    bias_part = hub_sum[WIDE * HUB : WIDE * HUB + HUB]
    hub_part[:, pl.ds(HUB, HUB), :] = jnp.broadcast_to(bias_part, (WIDE, HUB, TILE))
    send(hub_copy)
    hub_in[w] = hub_part[w]

    def add_own(i, c):
        at = pl.ds(i * TILE, TILE)
        acc[at, :] += slots[list_o[3, i]].T
        return c

    lax.fori_loop(0, DST, add_own, 0, unroll=4)
    lane = iota((1, TILE), 1)
    hub_lane = jnp.full((1, TILE), -1, I32)
    for j in range(HUB):
        hub_lane = jnp.where((lane == j) | (lane == j + HUB), hub_at[j], hub_lane)
    row_lane = jnp.concatenate([send_at[pl.ds(p, 1), :] for p in range(WIDE)], axis=1)
    step = 256
    base = iota((step, TILE), 0).astype(F32).astype(BF)
    one, zero = jnp.ones((), BF), jnp.zeros((), BF)

    def scatter(lanes, values, first, last):
        def add(i, c):
            at = pl.ds(i * step, step)
            near_by = jnp.clip(lanes - i * step, -1, step).astype(F32).astype(BF)
            hot = [
                jnp.where(base == near_by[:, c : c + TILE], one, zero)
                for c in range(0, lanes.shape[1], TILE)
            ]
            acc[at, :] += mm(jnp.concatenate(hot, axis=1), values)
            return c

        lax.fori_loop(first, last, add, 0, unroll=4)

    arrive(back_copy)
    pieces = DST * TILE // step
    returned = back[...].reshape(WIDE * SLOT, TILE)
    scatter(row_lane, returned, 0, pieces // 2)
    near_arrive(sum_near_copy)
    near = sum_near[0] + sum_near[1] + sum_near[2] + sum_near[3]
    part[...] = near.astype(BF)
    whole[w] = near.astype(BF)
    send(part_copy)
    scatter(row_lane, returned, pieces // 2, pieces)
    arrive(hub_copy)
    got = add_up(hub_in, 2 * HUB)
    mine = got[:HUB]
    total_bias[...] = got[HUB:]
    high = mine.astype(BF)
    low = (mine - high.astype(F32)).astype(BF)
    values = jnp.concatenate([high, low, jnp.zeros((TILE - 2 * HUB, TILE), BF)], axis=0)
    scatter(hub_lane, values, 0, pieces)
    arrive(part_copy)

    def sent(o, c):
        sum_copy(o, w).wait_send()
        hub_copy(o, w).wait_send()
        back_copy(o, w).wait_send()
        part_copy(o, w).wait_send()
        return c

    lax.fori_loop(1, WIDE, sent, 0)
    for k in range(1, NARROW):
        sum_near_copy(k, n).wait_send()
        hub_near_copy(k, n).wait_send()


def backward(list_o, hub_rows, send_rows, wbuf, w2, grad_pre, gt, sums, bound, hub_out):
    vmem = pl.BlockSpec(memory_space=pltpu.VMEM)
    hbm = pl.BlockSpec(memory_space=pltpu.HBM)
    dma = pltpu.SemaphoreType.DMA
    return pl.pallas_call(
        backward_kernel,
        out_shape=(
            pltpu.VMEM((DST * TILE, TILE), F32),
            pltpu.VMEM((WIDE, 16, TILE), BF),
            pltpu.VMEM((8, TILE), F32),
        ),
        in_specs=[hbm] * 3 + [vmem] * 7,
        out_specs=(vmem,) * 3,
        scratch_shapes=[
            pltpu.SMEM((4, SLOTS), I32),
            pltpu.SMEM((HUB,), I32),
            pltpu.VMEM((WIDE, SLOT), I32),
            pltpu.VMEM((PAIRS + 1, TILE, TILE), F32),
            pltpu.VMEM((WIDE, SLOT, TILE), BF),
            pltpu.VMEM((WIDE, 16, TILE), BF),
            pltpu.VMEM((WIDE, 2 * HUB, TILE), F32),
            pltpu.VMEM((16, TILE), F32),
            pltpu.VMEM((NARROW, 16, TILE), F32),
            pltpu.VMEM((NARROW, WIDE * HUB + 16, TILE), BF),
            pltpu.VMEM((WIDE, 2 * HUB, TILE), F32),
            pltpu.VMEM((16, TILE), BF),
            dma((WIDE,)), dma((WIDE,)), dma((WIDE,)), dma((WIDE,)),
            dma((WIDE,)), dma((WIDE,)), dma((WIDE,)), dma((WIDE,)),
            dma((NARROW,)), dma((NARROW,)), dma((NARROW,)), dma((NARROW,)), dma((3,)),
        ],
        compiler_params=pltpu.CompilerParams(
            collective_id=1, has_side_effects=True, vmem_limit_bytes=VMEM_LIMIT
        ),
    )(
        *map(in_hbm, (list_o, hub_rows, send_rows)),
        *map(in_vmem, (wbuf, w2, grad_pre, gt, sums, bound, hub_out)),
    )


def finish_kernel(acc, whole, total_bias, gfeat, g_self, g_neigh, g_bias, weights, bias, sem):
    store = pltpu.make_async_copy(acc, gfeat, sem.at[0])
    store.start()
    for p in range(WIDE):
        got = whole[p].astype(F32)
        weights[pl.ds(8 * p, 8), :] = jnp.concatenate([got[:8], got[8:]], axis=1)
    bias[...] = jnp.concatenate([total_bias[pl.ds(0, 1), :], total_bias[pl.ds(1, 1), :]], axis=1)
    outs = [
        pltpu.make_async_copy(weights.at[pl.ds(0, TILE)], g_self, sem.at[1]),
        pltpu.make_async_copy(weights.at[pl.ds(TILE, TILE)], g_neigh, sem.at[2]),
        pltpu.make_async_copy(bias, g_bias, sem.at[3]),
    ]
    for c in outs:
        c.start()
    for c in [store] + outs:
        c.wait()


def finish(acc, whole, total_bias):
    vmem = pl.BlockSpec(memory_space=pltpu.VMEM)
    hbm = pl.BlockSpec(memory_space=pltpu.HBM)
    return pl.pallas_call(
        finish_kernel,
        out_shape=(
            jax.ShapeDtypeStruct((DST * TILE, TILE), F32),
            jax.ShapeDtypeStruct((TILE, 2 * TILE), F32),
            jax.ShapeDtypeStruct((TILE, 2 * TILE), F32),
            jax.ShapeDtypeStruct((1, 2 * TILE), F32),
        ),
        in_specs=[vmem] * 3,
        out_specs=(hbm,) * 4,
        scratch_shapes=[
            pltpu.VMEM((2 * TILE, 2 * TILE), F32),
            pltpu.VMEM((1, 2 * TILE), F32),
            pltpu.SemaphoreType.DMA((4,)),
        ],
    )(in_vmem(acc), in_vmem(whole), in_vmem(total_bias))


def on_device(
    features, cotangent, w_self, w_neigh, bias, tile_weights, tile_src, tile_dst, tile_live,
    send_rows, hub_rows,
):
    lanes = (TILES // TILE, TILE)
    wbuf, buf, w2, b2, list_f, list_r, list_o = fetch(
        features.reshape(DST * QUADS, SLOT, TILE), w_self, w_neigh,
        bias.reshape(1, 2 * TILE), tile_weights,
        tile_src.reshape(lanes), tile_dst.reshape(lanes), tile_live.reshape(lanes),
        send_rows, hub_rows,
    )
    hidden, grad_pre, gt, sums, bound, hub_out = forward(
        list_f, list_r, cotangent, wbuf, buf, w2, b2
    )
    acc, whole, total_bias = backward(
        list_o, hub_rows, send_rows, wbuf, w2, grad_pre, gt, sums, bound, hub_out
    )
    grad_features, grad_self, grad_neigh, grad_bias = finish(acc, whole, total_bias)
    return (hidden, grad_features, grad_self, grad_neigh, grad_bias.reshape(2 * TILE))


def solution(mesh):
    both = ("wide", "narrow")
    placed = (
        P(both, None), P(both, None), P(), P(), P(), P(both, None, None),
        P(both), P(both), P(both), P(both, None), P(both),
    )
    return jax.shard_map(
        on_device,
        mesh=mesh,
        in_specs=placed,
        out_specs=(P(both, None), P(both, None), P(), P(), P()),
        check_vma=False,
    )
```

```python
import functools

import jax
import jax.numpy as jnp
from jax import lax
from jax.experimental import pallas as pl
from jax.experimental.pallas import tpu as pltpu
from jax.sharding import PartitionSpec as P

MESH = pl.DeviceIdType.MESH
BF, F32, I32 = jnp.bfloat16, jnp.float32, jnp.int32
TILE = 128
DST = 32
SRC = 48
TILES = 512
SLOTS = 640
UNROLL = 24
WALK = 34
PAIRS = 272
COUNT = 64
ROWS = 4096
CHUNKS = 8
FIRST = 6
VMEM_LIMIT = 32 * 2**20
SLOT = 32
QUADS = TILE // SLOT
HUB = 8
WIDE = 32
NARROW = 4
GELU_A = 0.7978845608028654
GELU_B = 0.044715


def mm(a, b):
    return jnp.dot(a, b, preferred_element_type=F32)


def nt(a, b):
    return lax.dot_general(a, b, (((1,), (1,)), ((), ())), preferred_element_type=F32)


def tn(a, b):
    return lax.dot_general(a, b, (((0,), (0,)), ((), ())), preferred_element_type=F32)


def iota(shape, dim):
    return lax.broadcasted_iota(I32, shape, dim)


def tile_list(key, other, live, keys, zero):
    groups = 64
    hot = jnp.where((iota((groups, TILES), 0) == key) & (live > 0), 1.0, 0.0)
    before = jnp.where(iota((TILES, TILES), 0) < iota((TILES, TILES), 1), 1.0, 0.0).astype(BF)
    rank = mm(hot.astype(BF), before)
    count = jnp.sum(hot, axis=1, keepdims=True).astype(I32)
    even = ((count + 1) // 2 * 2).astype(F32)
    lower = jnp.where(iota((groups, groups), 1) < iota((groups, groups), 0), 1.0, 0.0).astype(BF)
    start = mm(lower, jnp.broadcast_to(even, (groups, TILE)).astype(BF))[:, :1]
    total = jnp.sum(even, axis=0, keepdims=True)
    place = jnp.sum(hot * (rank + start), axis=0, keepdims=True).astype(I32)
    place = jnp.where(live > 0, place, -1)
    at = jnp.where(iota((SLOTS, TILES), 0) == place, 1.0, 0.0).astype(BF)
    t = iota((1, TILES), 1)
    rows = [t // 16, t % 16, other - zero, key - keys]
    row = iota((8, TILES), 0)
    values = jnp.zeros((8, TILES), I32)
    for r, v in enumerate(rows):
        values = jnp.where(row == r, v, values)
    got = nt(values.astype(F32).astype(BF), at).astype(I32)
    last = jnp.where(even > 0, (start + even) * 0.5 - 1.0, float(PAIRS))
    across = iota((groups, TILE), 0) == iota((groups, TILE), 1)
    last = jnp.sum(jnp.where(across, last, 0.0), axis=0, keepdims=True)
    info = jnp.where(iota((1, TILE), 1) < groups, last, total * 0.5).astype(I32)
    return jnp.concatenate(
        [
            got[0:1] * 16 + got[1:2],
            got[2:3] + zero,
            got[3:4] + keys,
            jnp.concatenate([info, jnp.zeros((1, SLOTS - TILE), I32)], axis=1),
        ],
        axis=0,
    )


def greet_all(w, n):
    barrier = pltpu.get_barrier_semaphore()

    def greet(o, c):
        pl.semaphore_signal(
            barrier, inc=1, device_id=(lax.rem(w + o, WIDE), n), device_id_type=MESH
        )
        return c

    lax.fori_loop(1, WIDE, greet, 0)
    for k in range(1, NARROW):
        pl.semaphore_signal(
            barrier, inc=1, device_id=(w, lax.rem(n + k, NARROW)), device_id_type=MESH
        )
    return barrier


def fetch_kernel(
    feat, w_self, w_neigh, bias, tiles, src, dst, live, send_rows, hub_rows,
    wbuf, buf, w2, b2, list_f, list_r, list_o,
    send_at, hub_at, keys, wide32, hubs, picked, msg, near, own, lists,
    s_row, r_row, s_hub, r_hub, s_near, r_near, s_own, s_in, s_big, s_list,
):
    w = lax.axis_index("wide")
    n = lax.axis_index("narrow")
    small = [
        pltpu.make_async_copy(send_rows, send_at, s_in.at[0]),
        pltpu.make_async_copy(hub_rows, hub_at, s_in.at[1]),
        pltpu.make_async_copy(feat, buf.at[pl.ds(0, DST * QUADS)], s_in.at[2]),
        pltpu.make_async_copy(src, keys.at[0], s_in.at[3]),
        pltpu.make_async_copy(dst, keys.at[1], s_in.at[4]),
        pltpu.make_async_copy(live, keys.at[2], s_in.at[5]),
    ]
    for c in small:
        c.start()
    barrier = greet_all(w, n)
    big = [
        pltpu.make_async_copy(w_self, w2.at[pl.ds(0, TILE)], s_big.at[0]),
        pltpu.make_async_copy(w_neigh, w2.at[pl.ds(TILE, TILE)], s_big.at[1]),
        pltpu.make_async_copy(bias, b2, s_big.at[2]),
    ]
    per = TILES // CHUNKS
    big += [
        pltpu.make_async_copy(
            tiles.at[pl.ds(i * per, per)], wbuf.at[pl.ds(i * per, per)], s_big.at[3 + i]
        )
        for i in range(CHUNKS)
    ]
    for c in big:
        c.start()
    buf[pl.ds(SRC * QUADS, QUADS)] = jnp.zeros((QUADS, SLOT, TILE), BF)
    for c in small[:3]:
        c.wait()
    wide32[...] = buf[pl.ds(0, DST * QUADS)].astype(F32).reshape(DST * TILE, TILE)
    for j in range(HUB):
        hubs[pl.ds(j, 1), :] = wide32[pl.ds(hub_at[j], 1), :]

    def pick(p, c):
        for j in range(SLOT):
            picked[pl.ds(p * SLOT + j, 1), :] = wide32[pl.ds(send_at[p, j], 1), :]
        return c

    lax.fori_loop(0, WIDE, pick, 0)
    msg[...] = picked[...].astype(BF).reshape(WIDE, SLOT, TILE)
    near[n] = hubs[...]

    pl.semaphore_wait(barrier, WIDE - 1 + NARROW - 1)
    rows_at, hubs_at = DST * QUADS, DST * QUADS + WIDE

    def near_copy(k, slot):
        return pltpu.make_async_remote_copy(
            src_ref=hubs,
            dst_ref=near.at[slot],
            send_sem=s_near.at[k],
            recv_sem=r_near.at[k],
            device_id=(w, lax.rem(n + k, NARROW)),
            device_id_type=MESH,
        )

    def row_copy(o, slot):
        p = lax.rem(w + o, WIDE)
        return pltpu.make_async_remote_copy(
            src_ref=msg.at[p],
            dst_ref=buf.at[rows_at + slot],
            send_sem=s_row.at[o],
            recv_sem=r_row.at[o],
            device_id=(p, n),
            device_id_type=MESH,
        )

    def hub_copy(o, slot):
        return pltpu.make_async_remote_copy(
            src_ref=own,
            dst_ref=buf.at[hubs_at + slot],
            send_sem=s_hub.at[o],
            recv_sem=r_hub.at[o],
            device_id=(lax.rem(w + o, WIDE), n),
            device_id_type=MESH,
        )

    for k in range(1, NARROW):
        near_copy(k, n).start()

    def send_row(o, c):
        row_copy(o, w).start()
        return c

    lax.fori_loop(1, WIDE, send_row, 0)
    mine_row = pltpu.make_async_copy(msg.at[w], buf.at[rows_at + w], s_own.at[0])
    mine_row.start()
    for k in range(1, NARROW):
        near_copy(k, lax.rem(n + NARROW - k, NARROW)).wait_recv()
    own[...] = near[...].reshape(NARROW * HUB, TILE).astype(BF)

    def send_hub(o, c):
        hub_copy(o, w).start()
        return c

    lax.fori_loop(1, WIDE, send_hub, 0)
    mine_hub = pltpu.make_async_copy(own, buf.at[hubs_at + w], s_own.at[1])
    mine_hub.start()

    for c in small[3:]:
        c.wait()

    def flat(i):
        return jnp.concatenate([keys[i, pl.ds(r, 1), :] for r in range(TILES // TILE)], axis=1)

    s, d, l = flat(0), flat(1), flat(2)
    lists[0] = tile_list(d, s, l, DST, SRC)
    lists[1] = tile_list(s - DST, d, jnp.where(s >= DST, l, 0), SRC - DST, DST)
    lists[2] = tile_list(s, d, jnp.where(s < DST, l, 0), DST, DST)
    out_lists = [
        pltpu.make_async_copy(lists.at[i], out, s_list.at[i])
        for i, out in enumerate((list_f, list_r, list_o))
    ]
    for c in out_lists:
        c.start()

    def finish(o, c):
        slot = lax.rem(w + WIDE - o, WIDE)
        row_copy(o, slot).wait()
        hub_copy(o, slot).wait()
        return c

    lax.fori_loop(1, WIDE, finish, 0)
    for k in range(1, NARROW):
        near_copy(k, n).wait_send()
    mine_row.wait()
    mine_hub.wait()
    for c in out_lists:
        c.wait()
    for c in big:
        c.wait()


def in_vmem(x):
    return pltpu.with_memory_space_constraint(x, pltpu.VMEM)


def in_hbm(x):
    return pltpu.with_memory_space_constraint(x, pltpu.HBM)


def fetch(*args):
    vmem = pl.BlockSpec(memory_space=pltpu.VMEM)
    hbm = pl.BlockSpec(memory_space=pltpu.HBM)
    dma = pltpu.SemaphoreType.DMA
    return pl.pallas_call(
        fetch_kernel,
        out_shape=(
            pltpu.VMEM((TILES, TILE, TILE), BF),
            pltpu.VMEM(((SRC + 1) * QUADS, SLOT, TILE), BF),
            pltpu.VMEM((2 * TILE, 2 * TILE), BF),
            pltpu.VMEM((1, 2 * TILE), F32),
            pltpu.HBM((4, SLOTS), I32),
            pltpu.HBM((4, SLOTS), I32),
            pltpu.HBM((4, SLOTS), I32),
        ),
        in_specs=[hbm] * 10,
        out_specs=(vmem,) * 4 + (hbm,) * 3,
        scratch_shapes=[
            pltpu.SMEM((WIDE, SLOT), I32),
            pltpu.SMEM((HUB,), I32),
            pltpu.VMEM((3, TILES // TILE, TILE), I32),
            pltpu.VMEM((DST * TILE, TILE), F32),
            pltpu.VMEM((HUB, TILE), F32),
            pltpu.VMEM((WIDE * SLOT, TILE), F32),
            pltpu.VMEM((WIDE, SLOT, TILE), BF),
            pltpu.VMEM((NARROW, HUB, TILE), F32),
            pltpu.VMEM((NARROW * HUB, TILE), BF),
            pltpu.VMEM((3, 4, SLOTS), I32),
            dma((WIDE,)), dma((WIDE,)), dma((WIDE,)), dma((WIDE,)),
            dma((NARROW,)), dma((NARROW,)), dma((2,)), dma((6,)), dma((3 + CHUNKS,)), dma((3,)),
        ],
        compiler_params=pltpu.CompilerParams(
            collective_id=0, has_side_effects=True, vmem_limit_bytes=VMEM_LIMIT
        ),
    )(*map(in_hbm, args))


def forward_kernel(
    lists_f, lists_r, cot, wbuf, buf, w2, bias, hidden, grad_pre, gt, sums, bound, hub_out,
    list_f, list_r, cotb, agg, hid, gbt, wg, gb, sem, s_hid,
):
    loads = [
        pltpu.make_async_copy(lists_f, list_f, sem.at[0]),
        pltpu.make_async_copy(lists_r, list_r, sem.at[1]),
        pltpu.make_async_copy(cot, cotb, sem.at[2]),
    ]
    for c in loads:
        c.start()

    def clear(i, c):
        agg[i] = jnp.zeros((TILE, TILE), F32)
        return c

    lax.fori_loop(0, DST + 1, clear, 0)
    loads[0].wait()

    def rows_of(s):
        return buf[pl.ds(s * QUADS, QUADS)].reshape(TILE, TILE)

    def step(i, c):
        parts = []
        for u in range(UNROLL):
            k = 2 * (i * UNROLL + u)
            left = jnp.concatenate([wbuf[list_f[0, k]], wbuf[list_f[0, k + 1]]], axis=1)
            right = jnp.concatenate(
                [rows_of(list_f[1, k]), rows_of(list_f[1, k + 1])], axis=0
            )
            parts.append(mm(left, right))
        for u in range(UNROLL):
            agg[list_f[2, 2 * (i * UNROLL + u)]] += parts[u]
        return c

    lax.fori_loop(0, (list_f[3, COUNT] + UNROLL - 1) // UNROLL, step, 0)
    def clear_back(i, c):
        gbt[i] = jnp.zeros((TILE, TILE), F32)
        return c

    lax.fori_loop(0, SRC - DST + 1, clear_back, 0)
    gb[...] = jnp.zeros_like(gb)
    wg[...] = jnp.zeros_like(wg)
    gt[DST] = jnp.zeros((TILE, TILE), BF)
    for c in loads[1:]:
        c.wait()
    blocks = ROWS // TILE

    def out_hidden(i):
        rows = pl.ds(i * ROWS, ROWS)
        return pltpu.make_async_copy(hid.at[rows, :], hidden.at[rows, :], s_hid.at[i])

    def activate(i, c):
        rows, at = pl.ds(i * ROWS, ROWS), pl.ds(i * blocks, blocks)
        f = buf[pl.ds(i * blocks * QUADS, blocks * QUADS)].reshape(ROWS, TILE)
        a = agg[at].reshape(ROWS, TILE).astype(BF)
        x = jnp.concatenate([f, a], axis=1)
        pre = mm(x, w2[...]) + bias[...]
        square = pre * pre
        t = jnp.tanh(pre * (GELU_A + (GELU_A * GELU_B) * square))
        half = 0.5 + 0.5 * t
        hid[rows, :] = (pre * half).astype(BF)
        out_hidden(i).start()
        slope = half + pre * (0.5 - 0.5 * t * t) * (GELU_A + (3 * GELU_A * GELU_B) * square)
        gp = (cotb[rows, :].astype(F32) * slope).astype(BF)
        grad_pre[rows, :] = gp
        wg[...] += tn(x, gp)
        gb[...] += jnp.sum(gp.astype(F32).reshape(ROWS // 8, 8, 2 * TILE), axis=0)
        g = nt(w2[pl.ds(TILE, TILE), :], gp).astype(BF)
        for j in range(blocks):
            gt[i * blocks + j] = g[:, j * TILE : (j + 1) * TILE]
        return c

    lax.fori_loop(0, DST // blocks, activate, 0)

    def step_back(i, c):
        parts = []
        for u in range(UNROLL):
            k = 2 * (i * UNROLL + u)
            left = jnp.concatenate([gt[list_r[1, k]], gt[list_r[1, k + 1]]], axis=1)
            right = jnp.concatenate([wbuf[list_r[0, k]], wbuf[list_r[0, k + 1]]], axis=0)
            parts.append(mm(left, right))
        for u in range(UNROLL):
            gbt[list_r[2, 2 * (i * UNROLL + u)]] += parts[u]
        return c

    lax.fori_loop(0, (list_r[3, COUNT] + UNROLL - 1) // UNROLL, step_back, 0)
    bias_sum = jnp.sum(gb[...], axis=0, keepdims=True)
    row = iota((16, TILE), 0)
    bias_rows = jnp.where(
        row == 0, bias_sum[:, :TILE], jnp.where(row == 1, bias_sum[:, TILE:], 0.0)
    ).astype(BF)
    for k in range(NARROW):
        hub_out[k, pl.ds(WIDE * HUB, 16), :] = bias_rows
    for p in range(WIDE):
        rows = wg[pl.ds(8 * p, 8), :]
        sums[p] = jnp.concatenate(
            [rows[:, :TILE], rows[:, TILE:]], axis=0
        ).astype(BF)
    remote = WIDE // QUADS
    for i in range(remote):
        at = pl.ds(i * QUADS, QUADS)
        bound[at] = gbt[i].T.astype(BF).reshape(QUADS, SLOT, TILE)
        total = gbt[remote + i].T
        for k in range(NARROW):
            rows = [total[q * SLOT + k * HUB :][:HUB] for q in range(QUADS)]
            hub_out[k, pl.ds(i * SLOT, SLOT), :] = jnp.concatenate(rows, axis=0).astype(BF)
    for i in range(DST // blocks):
        out_hidden(i).wait()


def forward(list_f, list_r, cot, wbuf, buf, w2, bias):
    vmem = pl.BlockSpec(memory_space=pltpu.VMEM)
    hbm = pl.BlockSpec(memory_space=pltpu.HBM)
    return pl.pallas_call(
        forward_kernel,
        out_shape=(
            jax.ShapeDtypeStruct((DST * TILE, 2 * TILE), BF),
            pltpu.VMEM((DST * TILE, 2 * TILE), BF),
            pltpu.VMEM((DST + 1, TILE, TILE), BF),
            pltpu.VMEM((WIDE, 16, TILE), BF),
            pltpu.VMEM((WIDE, SLOT, TILE), BF),
            pltpu.VMEM((NARROW, WIDE * HUB + 16, TILE), BF),
        ),
        in_specs=[hbm] * 3 + [vmem] * 4,
        out_specs=(hbm,) + (vmem,) * 5,
        scratch_shapes=[
            pltpu.SMEM((4, SLOTS), I32),
            pltpu.SMEM((4, SLOTS), I32),
            pltpu.VMEM((DST * TILE, 2 * TILE), BF),
            pltpu.VMEM((DST + 1, TILE, TILE), F32),
            pltpu.VMEM((DST * TILE, 2 * TILE), BF),
            pltpu.VMEM((SRC - DST + 1, TILE, TILE), F32),
            pltpu.VMEM((2 * TILE, 2 * TILE), F32),
            pltpu.VMEM((8, 2 * TILE), F32),
            pltpu.SemaphoreType.DMA((3,)),
            pltpu.SemaphoreType.DMA((DST * TILE // ROWS,)),
        ],
        compiler_params=pltpu.CompilerParams(vmem_limit_bytes=VMEM_LIMIT),
    )(*map(in_hbm, (list_f, list_r, cot)), *map(in_vmem, (wbuf, buf, w2, bias)))


def backward_kernel(
    lists_o, hub_rows, send_rows, wbuf, w2, grad_pre, gt, sums, bound, hub_out,
    acc, whole, total_bias,
    list_o, hub_at, send_at, slots, back, sum_in, hub_in, sum_out, sum_near, hub_near, hub_part,
    part, s_back, r_back, s_sum, r_sum, s_hub, r_hub, s_part, r_part,
    s_sum_near, r_sum_near, s_hub_near, r_hub_near, s_in,
):
    w = lax.axis_index("wide")
    n = lax.axis_index("narrow")
    loads = [
        pltpu.make_async_copy(lists_o, list_o, s_in.at[0]),
        pltpu.make_async_copy(hub_rows, hub_at, s_in.at[1]),
        pltpu.make_async_copy(send_rows, send_at, s_in.at[2]),
    ]
    for c in loads:
        c.start()
    barrier = greet_all(w, n)
    slots[PAIRS] = jnp.zeros((TILE, TILE), F32)

    pl.semaphore_wait(barrier, WIDE - 1 + NARROW - 1)

    def wide_copy(o, src, dst, send, recv):
        return pltpu.make_async_remote_copy(
            src_ref=src,
            dst_ref=dst,
            send_sem=send.at[o],
            recv_sem=recv.at[o],
            device_id=(lax.rem(w + o, WIDE), n),
            device_id_type=MESH,
        )

    def near_copy(k, src, dst, send, recv):
        return pltpu.make_async_remote_copy(
            src_ref=src,
            dst_ref=dst,
            send_sem=send.at[k],
            recv_sem=recv.at[k],
            device_id=(w, lax.rem(n + k, NARROW)),
            device_id_type=MESH,
        )

    def sum_copy(o, slot):
        return wide_copy(o, sums.at[lax.rem(w + o, WIDE)], sum_in.at[slot], s_sum, r_sum)

    def hub_copy(o, slot):
        return wide_copy(o, hub_part.at[lax.rem(w + o, WIDE)], hub_in.at[slot], s_hub, r_hub)

    def back_copy(o, slot):
        return wide_copy(o, bound.at[lax.rem(w + o, WIDE)], back.at[slot], s_back, r_back)

    def part_copy(o, slot):
        return wide_copy(o, part, whole.at[slot], s_part, r_part)

    def sum_near_copy(k, slot):
        return near_copy(k, sum_out, sum_near.at[slot], s_sum_near, r_sum_near)

    def hub_near_copy(k, slot):
        peer = lax.rem(n + k, NARROW)
        return near_copy(k, hub_out.at[peer], hub_near.at[slot], s_hub_near, r_hub_near)

    def send(copy):
        def one(o, c):
            copy(o, w).start()
            return c

        lax.fori_loop(1, WIDE, one, 0)

    def arrive(copy):
        def one(o, c):
            copy(o, lax.rem(w + WIDE - o, WIDE)).wait_recv()
            return c

        lax.fori_loop(1, WIDE, one, 0)

    def near_arrive(copy):
        for k in range(1, NARROW):
            copy(k, lax.rem(n + NARROW - k, NARROW)).wait_recv()

    def add_up(ref, rows):
        def one(q, total):
            return total + ref[q].astype(F32)

        return lax.fori_loop(0, WIDE, one, jnp.zeros((rows, TILE), F32), unroll=4)

    def walk(i, total):
        parts = []
        for u in range(WALK):
            k = 2 * (i * WALK + u)
            left = jnp.concatenate([gt[list_o[1, k]], gt[list_o[1, k + 1]]], axis=1)
            right = jnp.concatenate([wbuf[list_o[0, k]], wbuf[list_o[0, k + 1]]], axis=0)
            parts.append(mm(left, right))
        for u in range(WALK):
            k = i * WALK + u
            same = list_o[2, 2 * k] == list_o[2, jnp.maximum(2 * k - 2, 0)]
            total = total * same.astype(F32) + parts[u]
            slots[k] = total
        return total

    send(sum_copy)
    for k in range(1, NARROW):
        hub_near_copy(k, n).start()
    send(back_copy)
    sum_in[w] = sums[w]
    back[w] = bound[w]
    hub_near[n] = hub_out[n]
    for c in loads:
        c.wait()
    def own_part(i, c):
        rows = pl.ds(i * ROWS, ROWS)
        acc[rows, :] = nt(grad_pre[rows, :], w2[pl.ds(0, TILE), :])
        return c

    lax.fori_loop(0, DST * TILE // ROWS, own_part, 0)
    def add_own(i, c):
        at = pl.ds(i * TILE, TILE)
        acc[at, :] += slots[list_o[3, i]].T
        return c

    lane = iota((1, TILE), 1)
    hub_lane = jnp.full((1, TILE), -1, I32)
    for j in range(HUB):
        hub_lane = jnp.where((lane == j) | (lane == j + HUB), hub_at[j], hub_lane)
    row_lane = jnp.concatenate([send_at[pl.ds(p, 1), :] for p in range(WIDE)], axis=1)
    step = 256
    pieces = DST * TILE // step
    base = iota((step, TILE), 0).astype(F32).astype(BF)
    one, zero = jnp.ones((), BF), jnp.zeros((), BF)

    def scatter(lanes, values, first, last):
        def add(i, c):
            at = pl.ds(i * step, step)
            near_by = jnp.clip(lanes - i * step, -1, step).astype(F32).astype(BF)
            hot = [
                jnp.where(base == near_by[:, c : c + TILE], one, zero)
                for c in range(0, lanes.shape[1], TILE)
            ]
            acc[at, :] += mm(jnp.concatenate(hot, axis=1), values)
            return c

        lax.fori_loop(first, last, add, 0, unroll=4)

    def walk_on(first, last, total):
        return lax.fori_loop(first, last, walk, total)

    def own_sums():
        lax.fori_loop(0, DST, add_own, 0, unroll=4)

    def sums_arrived():
        arrive(sum_copy)
        sum_out[...] = add_up(sum_in, 16)
        sum_near[n] = sum_out[...]
        for k in range(1, NARROW):
            sum_near_copy(k, n).start()

    def hubs_near_by():
        near_arrive(hub_near_copy)
        hub_sum = sum(hub_near[k].astype(F32) for k in range(NARROW))
        hub_part[:, pl.ds(0, HUB), :] = hub_sum[: WIDE * HUB].reshape(WIDE, HUB, TILE)
        bias_part = hub_sum[WIDE * HUB : WIDE * HUB + HUB]
        hub_part[:, pl.ds(HUB, HUB), :] = jnp.broadcast_to(bias_part, (WIDE, HUB, TILE))
        send(hub_copy)
        hub_in[w] = hub_part[w]

    def sums_near_by():
        near_arrive(sum_near_copy)
        near = sum_near[0] + sum_near[1] + sum_near[2] + sum_near[3]
        part[...] = near.astype(BF)
        whole[w] = near.astype(BF)
        send(part_copy)

    def rows_back(first, last):
        scatter(row_lane, back[...].reshape(WIDE * SLOT, TILE), first, last)

    steps = PAIRS // WALK
    total = walk_on(0, FIRST, jnp.zeros((TILE, TILE), F32))
    sums_arrived()
    walk_on(FIRST, steps, total)
    hubs_near_by()
    own_sums()
    sums_near_by()
    arrive(back_copy)
    rows_back(0, pieces)
    arrive(hub_copy)
    got = add_up(hub_in, 2 * HUB)
    mine = got[:HUB]
    total_bias[...] = got[HUB:]
    high = mine.astype(BF)
    low = (mine - high.astype(F32)).astype(BF)
    values = jnp.concatenate([high, low, jnp.zeros((TILE - 2 * HUB, TILE), BF)], axis=0)
    scatter(hub_lane, values, 0, pieces)
    arrive(part_copy)

    def sent(o, c):
        sum_copy(o, w).wait_send()
        hub_copy(o, w).wait_send()
        back_copy(o, w).wait_send()
        part_copy(o, w).wait_send()
        return c

    lax.fori_loop(1, WIDE, sent, 0)
    for k in range(1, NARROW):
        sum_near_copy(k, n).wait_send()
        hub_near_copy(k, n).wait_send()


def backward(list_o, hub_rows, send_rows, wbuf, w2, grad_pre, gt, sums, bound, hub_out):
    vmem = pl.BlockSpec(memory_space=pltpu.VMEM)
    hbm = pl.BlockSpec(memory_space=pltpu.HBM)
    dma = pltpu.SemaphoreType.DMA
    return pl.pallas_call(
        backward_kernel,
        out_shape=(
            pltpu.VMEM((DST * TILE, TILE), F32),
            pltpu.VMEM((WIDE, 16, TILE), BF),
            pltpu.VMEM((8, TILE), F32),
        ),
        in_specs=[hbm] * 3 + [vmem] * 7,
        out_specs=(vmem,) * 3,
        scratch_shapes=[
            pltpu.SMEM((4, SLOTS), I32),
            pltpu.SMEM((HUB,), I32),
            pltpu.VMEM((WIDE, SLOT), I32),
            pltpu.VMEM((PAIRS + 1, TILE, TILE), F32),
            pltpu.VMEM((WIDE, SLOT, TILE), BF),
            pltpu.VMEM((WIDE, 16, TILE), BF),
            pltpu.VMEM((WIDE, 2 * HUB, TILE), F32),
            pltpu.VMEM((16, TILE), F32),
            pltpu.VMEM((NARROW, 16, TILE), F32),
            pltpu.VMEM((NARROW, WIDE * HUB + 16, TILE), BF),
            pltpu.VMEM((WIDE, 2 * HUB, TILE), F32),
            pltpu.VMEM((16, TILE), BF),
            dma((WIDE,)), dma((WIDE,)), dma((WIDE,)), dma((WIDE,)),
            dma((WIDE,)), dma((WIDE,)), dma((WIDE,)), dma((WIDE,)),
            dma((NARROW,)), dma((NARROW,)), dma((NARROW,)), dma((NARROW,)), dma((3,)),
        ],
        compiler_params=pltpu.CompilerParams(
            collective_id=1, has_side_effects=True, vmem_limit_bytes=VMEM_LIMIT
        ),
    )(
        *map(in_hbm, (list_o, hub_rows, send_rows)),
        *map(in_vmem, (wbuf, w2, grad_pre, gt, sums, bound, hub_out)),
    )


def finish_kernel(acc, whole, total_bias, gfeat, g_self, g_neigh, g_bias, weights, bias, sem):
    store = pltpu.make_async_copy(acc, gfeat, sem.at[0])
    store.start()
    for p in range(WIDE):
        got = whole[p].astype(F32)
        weights[pl.ds(8 * p, 8), :] = jnp.concatenate([got[:8], got[8:]], axis=1)
    bias[...] = jnp.concatenate([total_bias[pl.ds(0, 1), :], total_bias[pl.ds(1, 1), :]], axis=1)
    outs = [
        pltpu.make_async_copy(weights.at[pl.ds(0, TILE)], g_self, sem.at[1]),
        pltpu.make_async_copy(weights.at[pl.ds(TILE, TILE)], g_neigh, sem.at[2]),
        pltpu.make_async_copy(bias, g_bias, sem.at[3]),
    ]
    for c in outs:
        c.start()
    for c in [store] + outs:
        c.wait()


def finish(acc, whole, total_bias):
    vmem = pl.BlockSpec(memory_space=pltpu.VMEM)
    hbm = pl.BlockSpec(memory_space=pltpu.HBM)
    return pl.pallas_call(
        finish_kernel,
        out_shape=(
            jax.ShapeDtypeStruct((DST * TILE, TILE), F32),
            jax.ShapeDtypeStruct((TILE, 2 * TILE), F32),
            jax.ShapeDtypeStruct((TILE, 2 * TILE), F32),
            jax.ShapeDtypeStruct((1, 2 * TILE), F32),
        ),
        in_specs=[vmem] * 3,
        out_specs=(hbm,) * 4,
        scratch_shapes=[
            pltpu.VMEM((2 * TILE, 2 * TILE), F32),
            pltpu.VMEM((1, 2 * TILE), F32),
            pltpu.SemaphoreType.DMA((4,)),
        ],
    )(in_vmem(acc), in_vmem(whole), in_vmem(total_bias))


def on_device(
    features, cotangent, w_self, w_neigh, bias, tile_weights, tile_src, tile_dst, tile_live,
    send_rows, hub_rows,
):
    lanes = (TILES // TILE, TILE)
    wbuf, buf, w2, b2, list_f, list_r, list_o = fetch(
        features.reshape(DST * QUADS, SLOT, TILE), w_self, w_neigh,
        bias.reshape(1, 2 * TILE), tile_weights,
        tile_src.reshape(lanes), tile_dst.reshape(lanes), tile_live.reshape(lanes),
        send_rows, hub_rows,
    )
    hidden, grad_pre, gt, sums, bound, hub_out = forward(
        list_f, list_r, cotangent, wbuf, buf, w2, b2
    )
    acc, whole, total_bias = backward(
        list_o, hub_rows, send_rows, wbuf, w2, grad_pre, gt, sums, bound, hub_out
    )
    grad_features, grad_self, grad_neigh, grad_bias = finish(acc, whole, total_bias)
    return (hidden, grad_features, grad_self, grad_neigh, grad_bias.reshape(2 * TILE))


def solution(mesh):
    both = ("wide", "narrow")
    placed = (
        P(both, None), P(both, None), P(), P(), P(), P(both, None, None),
        P(both), P(both), P(both), P(both, None), P(both),
    )
    return jax.shard_map(
        on_device,
        mesh=mesh,
        in_specs=placed,
        out_specs=(P(both, None), P(both, None), P(), P(), P()),
        check_vma=False,
    )
```

```python
import functools

import jax
import jax.numpy as jnp
from jax import lax
from jax.experimental import pallas as pl
from jax.experimental.pallas import tpu as pltpu
from jax.sharding import PartitionSpec as P

MESH = pl.DeviceIdType.MESH
BF, F32, I32 = jnp.bfloat16, jnp.float32, jnp.int32
TILE = 128
DST = 32
SRC = 48
TILES = 512
SLOTS = 640
UNROLL = 24
WALK = 34
PAIRS = 272
COUNT = 64
ROWS = 4096
CHUNKS = 8
FIRST = 7
VMEM_LIMIT = 32 * 2**20
SLOT = 32
QUADS = TILE // SLOT
HUB = 8
WIDE = 32
NARROW = 4
GELU_A = 0.7978845608028654
GELU_B = 0.044715


def mm(a, b):
    return jnp.dot(a, b, preferred_element_type=F32)


def nt(a, b):
    return lax.dot_general(a, b, (((1,), (1,)), ((), ())), preferred_element_type=F32)


def tn(a, b):
    return lax.dot_general(a, b, (((0,), (0,)), ((), ())), preferred_element_type=F32)


def iota(shape, dim):
    return lax.broadcasted_iota(I32, shape, dim)


def tile_list(key, other, live, keys, zero):
    groups = 64
    hot = jnp.where((iota((groups, TILES), 0) == key) & (live > 0), 1.0, 0.0)
    before = jnp.where(iota((TILES, TILES), 0) < iota((TILES, TILES), 1), 1.0, 0.0).astype(BF)
    rank = mm(hot.astype(BF), before)
    count = jnp.sum(hot, axis=1, keepdims=True).astype(I32)
    even = ((count + 1) // 2 * 2).astype(F32)
    lower = jnp.where(iota((groups, groups), 1) < iota((groups, groups), 0), 1.0, 0.0).astype(BF)
    start = mm(lower, jnp.broadcast_to(even, (groups, TILE)).astype(BF))[:, :1]
    total = jnp.sum(even, axis=0, keepdims=True)
    place = jnp.sum(hot * (rank + start), axis=0, keepdims=True).astype(I32)
    place = jnp.where(live > 0, place, -1)
    at = jnp.where(iota((SLOTS, TILES), 0) == place, 1.0, 0.0).astype(BF)
    t = iota((1, TILES), 1)
    rows = [t // 16, t % 16, other - zero, key - keys]
    row = iota((8, TILES), 0)
    values = jnp.zeros((8, TILES), I32)
    for r, v in enumerate(rows):
        values = jnp.where(row == r, v, values)
    got = nt(values.astype(F32).astype(BF), at).astype(I32)
    last = jnp.where(even > 0, (start + even) * 0.5 - 1.0, float(PAIRS))
    across = iota((groups, TILE), 0) == iota((groups, TILE), 1)
    last = jnp.sum(jnp.where(across, last, 0.0), axis=0, keepdims=True)
    info = jnp.where(iota((1, TILE), 1) < groups, last, total * 0.5).astype(I32)
    return jnp.concatenate(
        [
            got[0:1] * 16 + got[1:2],
            got[2:3] + zero,
            got[3:4] + keys,
            jnp.concatenate([info, jnp.zeros((1, SLOTS - TILE), I32)], axis=1),
        ],
        axis=0,
    )


def greet_all(w, n):
    barrier = pltpu.get_barrier_semaphore()

    def greet(o, c):
        pl.semaphore_signal(
            barrier, inc=1, device_id=(lax.rem(w + o, WIDE), n), device_id_type=MESH
        )
        return c

    lax.fori_loop(1, WIDE, greet, 0)
    for k in range(1, NARROW):
        pl.semaphore_signal(
            barrier, inc=1, device_id=(w, lax.rem(n + k, NARROW)), device_id_type=MESH
        )
    return barrier


def fetch_kernel(
    feat, w_self, w_neigh, bias, tiles, src, dst, live, send_rows, hub_rows,
    wbuf, buf, w2, b2, list_f, list_r, list_o,
    send_at, hub_at, keys, wide32, hubs, picked, msg, near, own, lists,
    s_row, r_row, s_hub, r_hub, s_near, r_near, s_own, s_in, s_big, s_list,
):
    w = lax.axis_index("wide")
    n = lax.axis_index("narrow")
    small = [
        pltpu.make_async_copy(send_rows, send_at, s_in.at[0]),
        pltpu.make_async_copy(hub_rows, hub_at, s_in.at[1]),
        pltpu.make_async_copy(feat, buf.at[pl.ds(0, DST * QUADS)], s_in.at[2]),
        pltpu.make_async_copy(src, keys.at[0], s_in.at[3]),
        pltpu.make_async_copy(dst, keys.at[1], s_in.at[4]),
        pltpu.make_async_copy(live, keys.at[2], s_in.at[5]),
    ]
    for c in small:
        c.start()
    barrier = greet_all(w, n)
    big = [
        pltpu.make_async_copy(w_self, w2.at[pl.ds(0, TILE)], s_big.at[0]),
        pltpu.make_async_copy(w_neigh, w2.at[pl.ds(TILE, TILE)], s_big.at[1]),
        pltpu.make_async_copy(bias, b2, s_big.at[2]),
    ]
    per = TILES // CHUNKS
    big += [
        pltpu.make_async_copy(
            tiles.at[pl.ds(i * per, per)], wbuf.at[pl.ds(i * per, per)], s_big.at[3 + i]
        )
        for i in range(CHUNKS)
    ]
    for c in big:
        c.start()
    buf[pl.ds(SRC * QUADS, QUADS)] = jnp.zeros((QUADS, SLOT, TILE), BF)
    for c in small[:3]:
        c.wait()
    wide32[...] = buf[pl.ds(0, DST * QUADS)].astype(F32).reshape(DST * TILE, TILE)
    for j in range(HUB):
        hubs[pl.ds(j, 1), :] = wide32[pl.ds(hub_at[j], 1), :]

    def pick(p, c):
        for j in range(SLOT):
            picked[pl.ds(p * SLOT + j, 1), :] = wide32[pl.ds(send_at[p, j], 1), :]
        return c

    lax.fori_loop(0, WIDE, pick, 0)
    msg[...] = picked[...].astype(BF).reshape(WIDE, SLOT, TILE)
    near[n] = hubs[...]

    pl.semaphore_wait(barrier, WIDE - 1 + NARROW - 1)
    rows_at, hubs_at = DST * QUADS, DST * QUADS + WIDE

    def near_copy(k, slot):
        return pltpu.make_async_remote_copy(
            src_ref=hubs,
            dst_ref=near.at[slot],
            send_sem=s_near.at[k],
            recv_sem=r_near.at[k],
            device_id=(w, lax.rem(n + k, NARROW)),
            device_id_type=MESH,
        )

    def row_copy(o, slot):
        p = lax.rem(w + o, WIDE)
        return pltpu.make_async_remote_copy(
            src_ref=msg.at[p],
            dst_ref=buf.at[rows_at + slot],
            send_sem=s_row.at[o],
            recv_sem=r_row.at[o],
            device_id=(p, n),
            device_id_type=MESH,
        )

    def hub_copy(o, slot):
        return pltpu.make_async_remote_copy(
            src_ref=own,
            dst_ref=buf.at[hubs_at + slot],
            send_sem=s_hub.at[o],
            recv_sem=r_hub.at[o],
            device_id=(lax.rem(w + o, WIDE), n),
            device_id_type=MESH,
        )

    for k in range(1, NARROW):
        near_copy(k, n).start()

    def send_row(o, c):
        row_copy(o, w).start()
        return c

    lax.fori_loop(1, WIDE, send_row, 0)
    mine_row = pltpu.make_async_copy(msg.at[w], buf.at[rows_at + w], s_own.at[0])
    mine_row.start()
    for k in range(1, NARROW):
        near_copy(k, lax.rem(n + NARROW - k, NARROW)).wait_recv()
    own[...] = near[...].reshape(NARROW * HUB, TILE).astype(BF)

    def send_hub(o, c):
        hub_copy(o, w).start()
        return c

    lax.fori_loop(1, WIDE, send_hub, 0)
    mine_hub = pltpu.make_async_copy(own, buf.at[hubs_at + w], s_own.at[1])
    mine_hub.start()

    for c in small[3:]:
        c.wait()

    def flat(i):
        return jnp.concatenate([keys[i, pl.ds(r, 1), :] for r in range(TILES // TILE)], axis=1)

    s, d, l = flat(0), flat(1), flat(2)
    lists[0] = tile_list(d, s, l, DST, SRC)
    lists[1] = tile_list(s - DST, d, jnp.where(s >= DST, l, 0), SRC - DST, DST)
    lists[2] = tile_list(s, d, jnp.where(s < DST, l, 0), DST, DST)
    out_lists = [
        pltpu.make_async_copy(lists.at[i], out, s_list.at[i])
        for i, out in enumerate((list_f, list_r, list_o))
    ]
    for c in out_lists:
        c.start()

    def finish(o, c):
        slot = lax.rem(w + WIDE - o, WIDE)
        row_copy(o, slot).wait()
        hub_copy(o, slot).wait()
        return c

    lax.fori_loop(1, WIDE, finish, 0)
    for k in range(1, NARROW):
        near_copy(k, n).wait_send()
    mine_row.wait()
    mine_hub.wait()
    for c in out_lists:
        c.wait()
    for c in big:
        c.wait()


def in_vmem(x):
    return pltpu.with_memory_space_constraint(x, pltpu.VMEM)


def in_hbm(x):
    return pltpu.with_memory_space_constraint(x, pltpu.HBM)


def fetch(*args):
    vmem = pl.BlockSpec(memory_space=pltpu.VMEM)
    hbm = pl.BlockSpec(memory_space=pltpu.HBM)
    dma = pltpu.SemaphoreType.DMA
    return pl.pallas_call(
        fetch_kernel,
        out_shape=(
            pltpu.VMEM((TILES, TILE, TILE), BF),
            pltpu.VMEM(((SRC + 1) * QUADS, SLOT, TILE), BF),
            pltpu.VMEM((2 * TILE, 2 * TILE), BF),
            pltpu.VMEM((1, 2 * TILE), F32),
            pltpu.HBM((4, SLOTS), I32),
            pltpu.HBM((4, SLOTS), I32),
            pltpu.HBM((4, SLOTS), I32),
        ),
        in_specs=[hbm] * 10,
        out_specs=(vmem,) * 4 + (hbm,) * 3,
        scratch_shapes=[
            pltpu.SMEM((WIDE, SLOT), I32),
            pltpu.SMEM((HUB,), I32),
            pltpu.VMEM((3, TILES // TILE, TILE), I32),
            pltpu.VMEM((DST * TILE, TILE), F32),
            pltpu.VMEM((HUB, TILE), F32),
            pltpu.VMEM((WIDE * SLOT, TILE), F32),
            pltpu.VMEM((WIDE, SLOT, TILE), BF),
            pltpu.VMEM((NARROW, HUB, TILE), F32),
            pltpu.VMEM((NARROW * HUB, TILE), BF),
            pltpu.VMEM((3, 4, SLOTS), I32),
            dma((WIDE,)), dma((WIDE,)), dma((WIDE,)), dma((WIDE,)),
            dma((NARROW,)), dma((NARROW,)), dma((2,)), dma((6,)), dma((3 + CHUNKS,)), dma((3,)),
        ],
        compiler_params=pltpu.CompilerParams(
            collective_id=0, has_side_effects=True, vmem_limit_bytes=VMEM_LIMIT
        ),
    )(*map(in_hbm, args))


def forward_kernel(
    lists_f, lists_r, cot, wbuf, buf, w2, bias, hidden, grad_pre, gt, sums, bound, hub_out,
    list_f, list_r, cotb, agg, hid, gbt, wg, gb, sem, s_hid,
):
    loads = [
        pltpu.make_async_copy(lists_f, list_f, sem.at[0]),
        pltpu.make_async_copy(lists_r, list_r, sem.at[1]),
        pltpu.make_async_copy(cot, cotb, sem.at[2]),
    ]
    for c in loads:
        c.start()

    def clear(i, c):
        agg[i] = jnp.zeros((TILE, TILE), F32)
        return c

    lax.fori_loop(0, DST + 1, clear, 0)
    def clear_back(i, c):
        gbt[i] = jnp.zeros((TILE, TILE), F32)
        return c

    lax.fori_loop(0, SRC - DST + 1, clear_back, 0)
    gb[...] = jnp.zeros_like(gb)
    wg[...] = jnp.zeros_like(wg)
    gt[DST] = jnp.zeros((TILE, TILE), BF)
    loads[0].wait()

    def rows_of(s):
        return buf[pl.ds(s * QUADS, QUADS)].reshape(TILE, TILE)

    def step(i, c):
        parts = []
        for u in range(UNROLL):
            k = 2 * (i * UNROLL + u)
            left = jnp.concatenate([wbuf[list_f[0, k]], wbuf[list_f[0, k + 1]]], axis=1)
            right = jnp.concatenate(
                [rows_of(list_f[1, k]), rows_of(list_f[1, k + 1])], axis=0
            )
            parts.append(mm(left, right))
        for u in range(UNROLL):
            agg[list_f[2, 2 * (i * UNROLL + u)]] += parts[u]
        return c

    lax.fori_loop(0, (list_f[3, COUNT] + UNROLL - 1) // UNROLL, step, 0)
    for c in loads[1:]:
        c.wait()
    blocks = ROWS // TILE

    def out_hidden(i):
        rows = pl.ds(i * ROWS, ROWS)
        return pltpu.make_async_copy(hid.at[rows, :], hidden.at[rows, :], s_hid.at[i])

    def activate(i, c):
        rows, at = pl.ds(i * ROWS, ROWS), pl.ds(i * blocks, blocks)
        f = buf[pl.ds(i * blocks * QUADS, blocks * QUADS)].reshape(ROWS, TILE)
        a = agg[at].reshape(ROWS, TILE).astype(BF)
        x = jnp.concatenate([f, a], axis=1)
        pre = mm(x, w2[...]) + bias[...]
        square = pre * pre
        t = jnp.tanh(pre * (GELU_A + (GELU_A * GELU_B) * square))
        half = 0.5 + 0.5 * t
        hid[rows, :] = (pre * half).astype(BF)
        out_hidden(i).start()
        slope = half + pre * (0.5 - 0.5 * t * t) * (GELU_A + (3 * GELU_A * GELU_B) * square)
        gp = (cotb[rows, :].astype(F32) * slope).astype(BF)
        grad_pre[rows, :] = gp
        wg[...] += tn(x, gp)
        gb[...] += jnp.sum(gp.astype(F32).reshape(ROWS // 8, 8, 2 * TILE), axis=0)
        g = nt(w2[pl.ds(TILE, TILE), :], gp).astype(BF)
        for j in range(blocks):
            gt[i * blocks + j] = g[:, j * TILE : (j + 1) * TILE]
        return c

    lax.fori_loop(0, DST // blocks, activate, 0)

    def step_back(i, c):
        parts = []
        for u in range(UNROLL):
            k = 2 * (i * UNROLL + u)
            left = jnp.concatenate([gt[list_r[1, k]], gt[list_r[1, k + 1]]], axis=1)
            right = jnp.concatenate([wbuf[list_r[0, k]], wbuf[list_r[0, k + 1]]], axis=0)
            parts.append(mm(left, right))
        for u in range(UNROLL):
            gbt[list_r[2, 2 * (i * UNROLL + u)]] += parts[u]
        return c

    lax.fori_loop(0, (list_r[3, COUNT] + UNROLL - 1) // UNROLL, step_back, 0)
    bias_sum = jnp.sum(gb[...], axis=0, keepdims=True)
    row = iota((16, TILE), 0)
    bias_rows = jnp.where(
        row == 0, bias_sum[:, :TILE], jnp.where(row == 1, bias_sum[:, TILE:], 0.0)
    ).astype(BF)
    for k in range(NARROW):
        hub_out[k, pl.ds(WIDE * HUB, 16), :] = bias_rows
    for p in range(WIDE):
        rows = wg[pl.ds(8 * p, 8), :]
        sums[p] = jnp.concatenate(
            [rows[:, :TILE], rows[:, TILE:]], axis=0
        ).astype(BF)
    remote = WIDE // QUADS
    for i in range(remote):
        at = pl.ds(i * QUADS, QUADS)
        bound[at] = gbt[i].T.astype(BF).reshape(QUADS, SLOT, TILE)
        total = gbt[remote + i].T
        for k in range(NARROW):
            rows = [total[q * SLOT + k * HUB :][:HUB] for q in range(QUADS)]
            hub_out[k, pl.ds(i * SLOT, SLOT), :] = jnp.concatenate(rows, axis=0).astype(BF)
    for i in range(DST // blocks):
        out_hidden(i).wait()


def forward(list_f, list_r, cot, wbuf, buf, w2, bias):
    vmem = pl.BlockSpec(memory_space=pltpu.VMEM)
    hbm = pl.BlockSpec(memory_space=pltpu.HBM)
    return pl.pallas_call(
        forward_kernel,
        out_shape=(
            jax.ShapeDtypeStruct((DST * TILE, 2 * TILE), BF),
            pltpu.VMEM((DST * TILE, 2 * TILE), BF),
            pltpu.VMEM((DST + 1, TILE, TILE), BF),
            pltpu.VMEM((WIDE, 16, TILE), BF),
            pltpu.VMEM((WIDE, SLOT, TILE), BF),
            pltpu.VMEM((NARROW, WIDE * HUB + 16, TILE), BF),
        ),
        in_specs=[hbm] * 3 + [vmem] * 4,
        out_specs=(hbm,) + (vmem,) * 5,
        scratch_shapes=[
            pltpu.SMEM((4, SLOTS), I32),
            pltpu.SMEM((4, SLOTS), I32),
            pltpu.VMEM((DST * TILE, 2 * TILE), BF),
            pltpu.VMEM((DST + 1, TILE, TILE), F32),
            pltpu.VMEM((DST * TILE, 2 * TILE), BF),
            pltpu.VMEM((SRC - DST + 1, TILE, TILE), F32),
            pltpu.VMEM((2 * TILE, 2 * TILE), F32),
            pltpu.VMEM((8, 2 * TILE), F32),
            pltpu.SemaphoreType.DMA((3,)),
            pltpu.SemaphoreType.DMA((DST * TILE // ROWS,)),
        ],
        compiler_params=pltpu.CompilerParams(vmem_limit_bytes=VMEM_LIMIT),
    )(*map(in_hbm, (list_f, list_r, cot)), *map(in_vmem, (wbuf, buf, w2, bias)))


def backward_kernel(
    lists_o, hub_rows, send_rows, wbuf, w2, grad_pre, gt, sums, bound, hub_out,
    acc, whole, total_bias,
    list_o, hub_at, send_at, slots, back, sum_in, hub_in, sum_out, sum_near, hub_near, hub_part,
    part, s_back, r_back, s_sum, r_sum, s_hub, r_hub, s_part, r_part,
    s_sum_near, r_sum_near, s_hub_near, r_hub_near, s_in,
):
    w = lax.axis_index("wide")
    n = lax.axis_index("narrow")
    loads = [
        pltpu.make_async_copy(lists_o, list_o, s_in.at[0]),
        pltpu.make_async_copy(hub_rows, hub_at, s_in.at[1]),
        pltpu.make_async_copy(send_rows, send_at, s_in.at[2]),
    ]
    for c in loads:
        c.start()
    barrier = greet_all(w, n)
    slots[PAIRS] = jnp.zeros((TILE, TILE), F32)

    pl.semaphore_wait(barrier, WIDE - 1 + NARROW - 1)

    def wide_copy(o, src, dst, send, recv):
        return pltpu.make_async_remote_copy(
            src_ref=src,
            dst_ref=dst,
            send_sem=send.at[o],
            recv_sem=recv.at[o],
            device_id=(lax.rem(w + o, WIDE), n),
            device_id_type=MESH,
        )

    def near_copy(k, src, dst, send, recv):
        return pltpu.make_async_remote_copy(
            src_ref=src,
            dst_ref=dst,
            send_sem=send.at[k],
            recv_sem=recv.at[k],
            device_id=(w, lax.rem(n + k, NARROW)),
            device_id_type=MESH,
        )

    def sum_copy(o, slot):
        return wide_copy(o, sums.at[lax.rem(w + o, WIDE)], sum_in.at[slot], s_sum, r_sum)

    def hub_copy(o, slot):
        return wide_copy(o, hub_part.at[lax.rem(w + o, WIDE)], hub_in.at[slot], s_hub, r_hub)

    def back_copy(o, slot):
        return wide_copy(o, bound.at[lax.rem(w + o, WIDE)], back.at[slot], s_back, r_back)

    def part_copy(o, slot):
        return wide_copy(o, part, whole.at[slot], s_part, r_part)

    def sum_near_copy(k, slot):
        return near_copy(k, sum_out, sum_near.at[slot], s_sum_near, r_sum_near)

    def hub_near_copy(k, slot):
        peer = lax.rem(n + k, NARROW)
        return near_copy(k, hub_out.at[peer], hub_near.at[slot], s_hub_near, r_hub_near)

    def send(copy):
        def one(o, c):
            copy(o, w).start()
            return c

        lax.fori_loop(1, WIDE, one, 0)

    def arrive(copy):
        def one(o, c):
            copy(o, lax.rem(w + WIDE - o, WIDE)).wait_recv()
            return c

        lax.fori_loop(1, WIDE, one, 0)

    def near_arrive(copy):
        for k in range(1, NARROW):
            copy(k, lax.rem(n + NARROW - k, NARROW)).wait_recv()

    def add_up(ref, rows):
        def one(q, total):
            return total + ref[q].astype(F32)

        return lax.fori_loop(0, WIDE, one, jnp.zeros((rows, TILE), F32), unroll=4)

    def walk(i, total):
        parts = []
        for u in range(WALK):
            k = 2 * (i * WALK + u)
            left = jnp.concatenate([gt[list_o[1, k]], gt[list_o[1, k + 1]]], axis=1)
            right = jnp.concatenate([wbuf[list_o[0, k]], wbuf[list_o[0, k + 1]]], axis=0)
            parts.append(mm(left, right))
        for u in range(WALK):
            k = i * WALK + u
            same = list_o[2, 2 * k] == list_o[2, jnp.maximum(2 * k - 2, 0)]
            total = total * same.astype(F32) + parts[u]
            slots[k] = total
        return total

    send(sum_copy)
    for k in range(1, NARROW):
        hub_near_copy(k, n).start()
    send(back_copy)
    sum_in[w] = sums[w]
    back[w] = bound[w]
    hub_near[n] = hub_out[n]
    for c in loads:
        c.wait()
    def own_part(i, c):
        rows = pl.ds(i * ROWS, ROWS)
        acc[rows, :] = nt(grad_pre[rows, :], w2[pl.ds(0, TILE), :])
        return c

    lax.fori_loop(0, DST * TILE // ROWS, own_part, 0)
    def add_own(i, c):
        at = pl.ds(i * TILE, TILE)
        acc[at, :] += slots[list_o[3, i]].T
        return c

    lane = iota((1, TILE), 1)
    hub_lane = jnp.full((1, TILE), -1, I32)
    for j in range(HUB):
        hub_lane = jnp.where((lane == j) | (lane == j + HUB), hub_at[j], hub_lane)
    row_lane = jnp.concatenate([send_at[pl.ds(p, 1), :] for p in range(WIDE)], axis=1)
    step = 256
    pieces = DST * TILE // step
    base = iota((step, TILE), 0).astype(F32).astype(BF)
    one, zero = jnp.ones((), BF), jnp.zeros((), BF)

    def scatter(lanes, values, first, last):
        def add(i, c):
            at = pl.ds(i * step, step)
            near_by = jnp.clip(lanes - i * step, -1, step).astype(F32).astype(BF)
            hot = [
                jnp.where(base == near_by[:, c : c + TILE], one, zero)
                for c in range(0, lanes.shape[1], TILE)
            ]
            acc[at, :] += mm(jnp.concatenate(hot, axis=1), values)
            return c

        lax.fori_loop(first, last, add, 0, unroll=4)

    def walk_on(first, last, total):
        return lax.fori_loop(first, last, walk, total)

    def own_sums():
        lax.fori_loop(0, DST, add_own, 0, unroll=4)

    def sums_arrived():
        arrive(sum_copy)
        sum_out[...] = add_up(sum_in, 16)
        sum_near[n] = sum_out[...]
        for k in range(1, NARROW):
            sum_near_copy(k, n).start()

    def hubs_near_by():
        near_arrive(hub_near_copy)
        hub_sum = sum(hub_near[k].astype(F32) for k in range(NARROW))
        hub_part[:, pl.ds(0, HUB), :] = hub_sum[: WIDE * HUB].reshape(WIDE, HUB, TILE)
        bias_part = hub_sum[WIDE * HUB : WIDE * HUB + HUB]
        hub_part[:, pl.ds(HUB, HUB), :] = jnp.broadcast_to(bias_part, (WIDE, HUB, TILE))
        send(hub_copy)
        hub_in[w] = hub_part[w]

    def sums_near_by():
        near_arrive(sum_near_copy)
        near = sum_near[0] + sum_near[1] + sum_near[2] + sum_near[3]
        part[...] = near.astype(BF)
        whole[w] = near.astype(BF)
        send(part_copy)

    def rows_back(first, last):
        scatter(row_lane, back[...].reshape(WIDE * SLOT, TILE), first, last)

    steps = PAIRS // WALK
    total = walk_on(0, FIRST, jnp.zeros((TILE, TILE), F32))
    sums_arrived()
    walk_on(FIRST, steps, total)
    hubs_near_by()
    own_sums()
    sums_near_by()
    arrive(back_copy)
    rows_back(0, pieces)
    arrive(hub_copy)
    got = add_up(hub_in, 2 * HUB)
    mine = got[:HUB]
    total_bias[...] = got[HUB:]
    high = mine.astype(BF)
    low = (mine - high.astype(F32)).astype(BF)
    values = jnp.concatenate([high, low, jnp.zeros((TILE - 2 * HUB, TILE), BF)], axis=0)
    scatter(hub_lane, values, 0, pieces)
    arrive(part_copy)

    def sent(o, c):
        sum_copy(o, w).wait_send()
        hub_copy(o, w).wait_send()
        back_copy(o, w).wait_send()
        part_copy(o, w).wait_send()
        return c

    lax.fori_loop(1, WIDE, sent, 0)
    for k in range(1, NARROW):
        sum_near_copy(k, n).wait_send()
        hub_near_copy(k, n).wait_send()


def backward(list_o, hub_rows, send_rows, wbuf, w2, grad_pre, gt, sums, bound, hub_out):
    vmem = pl.BlockSpec(memory_space=pltpu.VMEM)
    hbm = pl.BlockSpec(memory_space=pltpu.HBM)
    dma = pltpu.SemaphoreType.DMA
    return pl.pallas_call(
        backward_kernel,
        out_shape=(
            pltpu.VMEM((DST * TILE, TILE), F32),
            pltpu.VMEM((WIDE, 16, TILE), BF),
            pltpu.VMEM((8, TILE), F32),
        ),
        in_specs=[hbm] * 3 + [vmem] * 7,
        out_specs=(vmem,) * 3,
        scratch_shapes=[
            pltpu.SMEM((4, SLOTS), I32),
            pltpu.SMEM((HUB,), I32),
            pltpu.VMEM((WIDE, SLOT), I32),
            pltpu.VMEM((PAIRS + 1, TILE, TILE), F32),
            pltpu.VMEM((WIDE, SLOT, TILE), BF),
            pltpu.VMEM((WIDE, 16, TILE), BF),
            pltpu.VMEM((WIDE, 2 * HUB, TILE), F32),
            pltpu.VMEM((16, TILE), F32),
            pltpu.VMEM((NARROW, 16, TILE), F32),
            pltpu.VMEM((NARROW, WIDE * HUB + 16, TILE), BF),
            pltpu.VMEM((WIDE, 2 * HUB, TILE), F32),
            pltpu.VMEM((16, TILE), BF),
            dma((WIDE,)), dma((WIDE,)), dma((WIDE,)), dma((WIDE,)),
            dma((WIDE,)), dma((WIDE,)), dma((WIDE,)), dma((WIDE,)),
            dma((NARROW,)), dma((NARROW,)), dma((NARROW,)), dma((NARROW,)), dma((3,)),
        ],
        compiler_params=pltpu.CompilerParams(
            collective_id=1, has_side_effects=True, vmem_limit_bytes=VMEM_LIMIT
        ),
    )(
        *map(in_hbm, (list_o, hub_rows, send_rows)),
        *map(in_vmem, (wbuf, w2, grad_pre, gt, sums, bound, hub_out)),
    )


def finish_kernel(acc, whole, total_bias, gfeat, g_self, g_neigh, g_bias, weights, bias, sem):
    store = pltpu.make_async_copy(acc, gfeat, sem.at[0])
    store.start()
    for p in range(WIDE):
        got = whole[p].astype(F32)
        weights[pl.ds(8 * p, 8), :] = jnp.concatenate([got[:8], got[8:]], axis=1)
    bias[...] = jnp.concatenate([total_bias[pl.ds(0, 1), :], total_bias[pl.ds(1, 1), :]], axis=1)
    outs = [
        pltpu.make_async_copy(weights.at[pl.ds(0, TILE)], g_self, sem.at[1]),
        pltpu.make_async_copy(weights.at[pl.ds(TILE, TILE)], g_neigh, sem.at[2]),
        pltpu.make_async_copy(bias, g_bias, sem.at[3]),
    ]
    for c in outs:
        c.start()
    for c in [store] + outs:
        c.wait()


def finish(acc, whole, total_bias):
    vmem = pl.BlockSpec(memory_space=pltpu.VMEM)
    hbm = pl.BlockSpec(memory_space=pltpu.HBM)
    return pl.pallas_call(
        finish_kernel,
        out_shape=(
            jax.ShapeDtypeStruct((DST * TILE, TILE), F32),
            jax.ShapeDtypeStruct((TILE, 2 * TILE), F32),
            jax.ShapeDtypeStruct((TILE, 2 * TILE), F32),
            jax.ShapeDtypeStruct((1, 2 * TILE), F32),
        ),
        in_specs=[vmem] * 3,
        out_specs=(hbm,) * 4,
        scratch_shapes=[
            pltpu.VMEM((2 * TILE, 2 * TILE), F32),
            pltpu.VMEM((1, 2 * TILE), F32),
            pltpu.SemaphoreType.DMA((4,)),
        ],
    )(in_vmem(acc), in_vmem(whole), in_vmem(total_bias))


def on_device(
    features, cotangent, w_self, w_neigh, bias, tile_weights, tile_src, tile_dst, tile_live,
    send_rows, hub_rows,
):
    lanes = (TILES // TILE, TILE)
    wbuf, buf, w2, b2, list_f, list_r, list_o = fetch(
        features.reshape(DST * QUADS, SLOT, TILE), w_self, w_neigh,
        bias.reshape(1, 2 * TILE), tile_weights,
        tile_src.reshape(lanes), tile_dst.reshape(lanes), tile_live.reshape(lanes),
        send_rows, hub_rows,
    )
    hidden, grad_pre, gt, sums, bound, hub_out = forward(
        list_f, list_r, cotangent, wbuf, buf, w2, b2
    )
    acc, whole, total_bias = backward(
        list_o, hub_rows, send_rows, wbuf, w2, grad_pre, gt, sums, bound, hub_out
    )
    grad_features, grad_self, grad_neigh, grad_bias = finish(acc, whole, total_bias)
    return (hidden, grad_features, grad_self, grad_neigh, grad_bias.reshape(2 * TILE))


def solution(mesh):
    both = ("wide", "narrow")
    placed = (
        P(both, None), P(both, None), P(), P(), P(), P(both, None, None),
        P(both), P(both), P(both), P(both, None), P(both),
    )
    return jax.shard_map(
        on_device,
        mesh=mesh,
        in_specs=placed,
        out_specs=(P(both, None), P(both, None), P(), P(), P()),
        check_vma=False,
    )
```
